256 devices in a mesh: cache: 4 (over y), ctx: 32 (over z, x), head: 2 (over core).
Axes of the slice: x: 4, y: 4, z: 8, core: 2. Of those that a mesh axis runs over, the one named last changes fastest.
Arguments:
- conv_out: bfloat16 [8, 2048, 16384], P('cache', 'ctx', 'head'), may hold values from -6 to 6
- dt_low: bfloat16 [8, 2048, 512], P('cache', 'ctx'), may hold values from -6 to 6
- state_proj: float32 [8, 2048, 32], P('cache', 'ctx'), may hold values from -1.2 to 1.2
- dt_weight: bfloat16 [512, 16384], P('ctx', 'head'), may hold values from -0.25 to 0.25
- dt_bias: float32 [16384], P('head'), may hold values from -2.5 to -0.5
- decay_rate: float32 [16, 16384], P(None, 'head'), may hold values from 0.0003 to 0.15
- skip_gain: float32 [16384], P('head'), may hold values from 0.5 to 1.5
- cache_states: bfloat16 [256, 2, 16, 8192], P('cache', 'head', None, 'ctx'), may hold values from -10 to 10
- hit_owner: int32 [8, 1], replicated, may hold values from 0 to 3; in each aligned block of 2 rows (0 to 1, 2 to 3, ...) at most 2 rows name the same one
- hit_slot: int32 [8], replicated, may hold values from 0 to 63
- evict_order: int32 [4, 64], P('cache'), may hold values from 0 to 63, each once within a row
- new_lengths: int32 [8], replicated, may hold values from 1 to 2048, 10240 in all
Outputs:
- mixed_out: bfloat16 [8, 2048, 16384], P('cache', 'ctx', 'head')
- new_cache: bfloat16 [256, 2, 16, 8192], P('cache', 'head', None, 'ctx')
The draws below stay inside these ranges and needn't reach their ends.
Inputs may be any that keep to these rules, and one draw needn't show every extreme that they name: `hit_owner`: among the 2 requests of one index of cache (aligned blocks of 2), no owner is named more than 2 times. `evict_order`: each row holds every slot number once. `new_lengths`: the longest request has exactly 2048 new positions.
All inputs are finite; a program needn't handle non-finite values.
Results may differ from the reference program's by a relative error of at most 0.0085.
Values may be sent and summed in bfloat16 or wider, within the bound.
No kernel may reach another device: no remote copies, remote signals or barrier semaphores. Data moves between devices by JAX's collectives and lax.ppermute only.
A program may use at most 192 MiB of HBM per device.

```python
import math
import jax
import jax.numpy as jnp
import numpy as np
from jax import lax

DI = 16384
N = 16
DT_RANK = 512
R_DEV = 2
S_OWN = 64
MOST = 2
REQUESTS = 8
CTX_LEN = 2048
OWNERS = 4
CACHE_SLOTS = 256
HALVES = 2
HEAD_CH = 8192
NBC = 32
N_CACHE = 4


def plant(values, key, low, largest):
    spot = [jax.random.randint(jax.random.fold_in(key, axis), (), 0, length) for axis, length in enumerate(values.shape)]
    widest = values.shape.index(max(values.shape))
    next_to = spot[:widest] + [(spot[widest] + 1) % values.shape[widest]] + spot[widest + 1:]
    return values.at[tuple(spot)].set(low).at[tuple(next_to)].set(largest)


def shard_levels(stream_key, dims, shards, low, largest):
    loudness = 1.0
    for position, shards_of in shards:
        draws = jax.random.uniform(jax.random.fold_in(jax.random.fold_in(stream_key, 6), position), (shards_of,), jnp.float32, low / len(shards), largest / len(shards))
        loudness = loudness * jnp.repeat(jnp.exp(draws), dims[position] // shards_of).reshape((-1,) + (1,) * (len(dims) - 1 - position))
    return loudness


def length_profile(number_of, total, most, skew):
    weights = [(1 << 20) // math.isqrt(rank ** skew) + 1 for rank in range(2, number_of + 1)]
    spare, holding = total - most - (number_of - 1), [1] * (number_of - 1)
    while spare > 0:
        candidates = [i for i in range(number_of - 1) if holding[i] < most]
        pool, remaining = sum([weights[i] for i in candidates]), spare
        for i in candidates:
            addition = min(most - holding[i], max(1, remaining * weights[i] // pool), spare)
            holding[i] = holding[i] + addition
            spare = spare - addition
    return np.array([most] + holding)


def uneven(stream_key, count, total, bound, skew):
    if count == 2:
        one = jax.random.randint(stream_key, (), max(1, total - bound), min(bound, total - 1) + 1)
        return jnp.stack([one, total - one])
    tallies = jnp.asarray(length_profile(count, total, bound, skew), jnp.int32)
    couples = (count - 1) // 2
    giver, sink = tallies[1:1 + 2 * couples:2], tallies[2:2 + 2 * couples:2]
    room = jnp.minimum(giver - 1, bound - sink)
    moved = jax.random.randint(jax.random.fold_in(stream_key, 1), (couples,), 0, 1 << 20) % (room + 1)
    tallies = tallies.at[1:1 + 2 * couples:2].set(giver - moved).at[2:2 + 2 * couples:2].set(sink + moved)
    return tallies[jax.random.permutation(jax.random.fold_in(stream_key, 2), count)]


def shared_out(key, own, number, rows, amount, top, limit, lean):
    order = jax.random.permutation(key, amount)
    crowded, usual = shares(amount, rows * top, limit, lean, True), shares(amount, rows * top, limit, lean, False)
    places = jnp.arange(amount)

    def named(tallies, rotation):
        used = int((tallies > 0).sum())
        fixed = max(1, used // 4)
        moved = fixed + (places - fixed + rotation * (used - fixed)) % max(1, amount - fixed)
        return jnp.zeros((amount,), jnp.int32).at[order[jnp.where(places < fixed, places, moved)]].set(jnp.asarray(tallies, jnp.int32))

    tallies = jnp.where(number % 4 == 0, named(crowded, number // 4), named(usual, number - number // 4 - 1))
    mixed = jax.random.permutation(jax.random.fold_in(own, 3), amount)
    donor, taker = mixed[0:amount // 2 * 2:2], mixed[1:amount // 2 * 2:2]
    slack = jnp.minimum(tallies[donor] - 1, limit - tallies[taker]) // 2
    slack = jnp.where((donor == order[0]) | (taker == order[0]) | (tallies[taker] == 0), 0, jnp.maximum(slack, 0))
    moved = jax.random.randint(jax.random.fold_in(own, 4), (amount // 2,), 0, 1 << 20) % (slack + 1)
    tallies = tallies.at[donor].add(-moved).at[taker].add(moved)
    labels = jnp.searchsorted(jnp.cumsum(tallies), jnp.arange(rows * top), side="right").astype(jnp.int32)
    listing = labels.reshape(top, rows).T
    listing = listing[jax.random.permutation(jax.random.fold_in(own, 1), rows)]
    rotation = jax.random.randint(jax.random.fold_in(own, 2), (rows, 1), 0, top)
    return jnp.take_along_axis(listing, (jnp.arange(top)[None, :] + rotation) % top, axis=1)


def shares(count, total, most, lean, full):
    loads = [(1 << 20) // math.isqrt(rank ** lean) + 1 for rank in range(1, count + 1)]
    largest = most if full else min(most, max(-(-total // count), total * loads[0] // sum(loads)))
    least = 1 if total - largest >= count - 1 else 0
    given, rest = [largest] + [least] * (count - 1), total - largest - least * (count - 1)
    while rest > 0:
        candidates = [i for i in range(1, count) if given[i] < largest] or [i for i in range(1, count) if given[i] < most]
        mass, remaining = sum([loads[i] for i in candidates]), rest
        for i in candidates:
            more = min(most - given[i], max(1, remaining * loads[i] // mass), rest)
            given[i] = given[i] + more
            rest = rest - more
    return np.array(given)


def scatter_about(key, extent, width, reach, pieces=(), kind=jnp.bfloat16):
    array = width * jax.random.normal(key, extent, jnp.float32)
    if pieces:
        array = array * shard_levels(key, extent, pieces, -0.22, 0.18)
    return jnp.clip(array, -reach, reach).astype(kind)


def setup_inputs(seed: int = 0) -> dict:
    streams_of = jax.random.split(jax.random.key(seed), 13)
    conv_out = scatter_about(streams_of[0], (REQUESTS, CTX_LEN, DI), 1.0, 6.0, ((0, 4), (1, 32), (2, 2)))
    dt_low = scatter_about(streams_of[1], (REQUESTS, CTX_LEN, DT_RANK), 1.0, 6.0, ((0, 4), (1, 32)))
    state_proj = scatter_about(streams_of[2], (REQUESTS, CTX_LEN, NBC), 0.2, 1.2, ((0, 4), (1, 32)), jnp.float32)
    dt_weight = scatter_about(streams_of[3], (DT_RANK, DI), DT_RANK ** -0.5, 0.25, ((0, 32), (1, 2)))
    dt_bias = jnp.clip(-2.5 + 2.0 * jax.random.uniform(streams_of[4], (DI,), jnp.float32) ** shard_levels(streams_of[4], (DI,), ((0, 2),), -0.2, 0.2), -2.5, -0.5)
    decay_rate = jnp.clip(jnp.exp(math.log(0.15) - 6.214608 * jax.random.uniform(streams_of[5], (N, DI), jnp.float32) ** shard_levels(streams_of[5], (N, DI), ((1, 2),), -0.2, 0.2)), 0.0003, 0.15)
    skip_gain = jnp.clip(1.0 + 0.1 * jax.random.normal(streams_of[6], (DI,), jnp.float32), 0.5, 1.5)
    cache_states = scatter_about(streams_of[7], (CACHE_SLOTS, HALVES, N, HEAD_CH), 2.0, 10.0, ((0, 4), (1, 2), (3, 32)))
    hit_owner_keys = jax.random.split(jax.random.fold_in(streams_of[8], 1), REQUESTS // R_DEV)
    hit_owner_turns = jax.random.permutation(jax.random.fold_in(streams_of[8], 3), REQUESTS // R_DEV)
    hit_owner = jax.vmap(lambda own, number: shared_out(jax.random.fold_in(streams_of[8], 2), own, number, R_DEV, N_CACHE, 1, MOST, 0))(hit_owner_keys, hit_owner_turns).reshape((REQUESTS, 1))
    hit_slot = plant(jax.random.randint(streams_of[9], (REQUESTS,), 0, S_OWN), jax.random.fold_in(streams_of[9], 1), 0, S_OWN - 1).astype(jnp.int32)
    evict_order = jax.vmap(lambda own: jax.random.permutation(own, S_OWN))(jax.random.split(streams_of[10], OWNERS)).reshape((OWNERS, S_OWN)).astype(jnp.int32)
    new_lengths = uneven(streams_of[11], REQUESTS, REQUESTS * CTX_LEN * 5 // 8, CTX_LEN, 2).astype(jnp.int32)
    return dict(conv_out=conv_out, dt_low=dt_low, state_proj=state_proj, dt_weight=dt_weight, dt_bias=dt_bias, decay_rate=decay_rate, skip_gain=skip_gain, cache_states=cache_states, hit_owner=hit_owner, hit_slot=hit_slot, evict_order=evict_order, new_lengths=new_lengths)


def reference(conv_out, dt_low, state_proj, dt_weight, dt_bias, decay_rate, skip_gain, cache_states, hit_owner, hit_slot, evict_order, new_lengths):
    owners = hit_owner[:, 0]
    positions = jnp.arange(CTX_LEN, dtype=jnp.int32)

    def one_request(request):
        slot_index = (owners[request] * S_OWN + hit_slot[request]).astype(jnp.int32)
        stored_block = lax.dynamic_index_in_dim(cache_states, slot_index, 0, keepdims=False).astype(jnp.float32)
        start_state = jnp.transpose(stored_block, (1, 0, 2)).reshape(N, DI)
        live_mask = positions < new_lengths[request]
        pre_rate = jnp.dot(dt_low[request], dt_weight, preferred_element_type=jnp.float32)
        step_rate = jnp.where(live_mask[:, None], jax.nn.softplus(pre_rate + dt_bias[None, :]), jnp.float32(0.0))

        def advance(carried, inputs):
            step_now, token_x, proj_now, live_now = inputs
            wide_x = token_x.astype(jnp.float32)
            carried = jnp.exp(-step_now[None, :] * decay_rate) * carried + proj_now[:N, None] * (step_now * wide_x)[None, :]
            output_row = jnp.dot(proj_now[N:], carried, precision=lax.Precision.HIGHEST) + skip_gain * wide_x
            return carried, jnp.where(live_now, output_row, jnp.float32(0.0)).astype(jnp.bfloat16)

        final_state, rows_out = lax.scan(advance, start_state, (step_rate, conv_out[request], state_proj[request], live_mask))
        return rows_out, final_state.astype(jnp.bfloat16)

    mixed_out, finals = lax.map(one_request, jnp.arange(REQUESTS, dtype=jnp.int32))
    request_ids = jnp.arange(REQUESTS, dtype=jnp.int32)
    same_owner = owners[:, None] == owners[None, :]
    ranks = jnp.sum(same_owner & (request_ids[None, :] < request_ids[:, None]), axis=1).astype(jnp.int32)
    targets = (owners * S_OWN + evict_order[owners, ranks]).astype(jnp.int32)
    blocks = jnp.transpose(finals.reshape(REQUESTS, N, HALVES, HEAD_CH), (0, 2, 1, 3))
    new_cache = cache_states.at[targets].set(blocks)
    return mixed_out, new_cache
```

```python
import math

import jax
import jax.numpy as jnp
from jax import lax
from jax.experimental import pallas as pl
from jax.experimental.pallas import tpu as pltpu
from jax.sharding import Mesh, PartitionSpec as P

HI, LO = 4, 8
LANES, ROWS = 128, 8
LOG2E = math.log2(math.e)


def scan_kernel(
    place_ref, proj_ref, x_ref, dt_ref, w_ref, bias_ref, decay_ref, skip_ref, start_ref,
    y_ref, total_ref, end_ref, step_scr, x_scr,
):
    parts, reqs, toks, chans = x_ref.shape
    states = decay_ref.shape[0]
    rows = reqs * toks
    nbc = proj_ref.shape[0] // (parts * rows)

    def project(part, carry):
        wide_x = x_ref[part].reshape(rows, chans).astype(jnp.float32)
        pre = jnp.dot(
            dt_ref[part].reshape(rows, -1), w_ref[...], preferred_element_type=jnp.float32
        )
        pre = pre + bias_ref[...]
        row = lax.broadcasted_iota(jnp.int32, (rows, 1), 0)
        position = place_ref[0] + part * toks + jnp.where(row < toks, row, row - toks)
        limit = jnp.where(row < toks, place_ref[1], place_ref[2])
        step = jnp.maximum(pre, 0.0) + jnp.log1p(jnp.exp(-jnp.abs(pre)))
        step = jnp.where(position < limit, step, 0.0)
        for k in range(ROWS):
            at = pl.ds(part * (rows * ROWS) + k, rows, stride=ROWS)
            step_scr[at, :] = step[:, k * LANES : (k + 1) * LANES]
            x_scr[at, :] = wide_x[:, k * LANES : (k + 1) * LANES]
        return carry

    lax.fori_loop(0, parts, project, 0)

    skip = skip_ref[...]
    for req in range(reqs):

        def per_part(part, carried, req=req):
            def per_tok(tok, carried):
                total, held = carried
                row = (part * reqs + req) * toks + tok
                at = pl.ds(pl.multiple_of(row * ROWS, ROWS), ROWS)
                step = step_scr[at, :]
                wide_x = x_scr[at, :]
                driven = step * wide_x
                total = total + step
                out = skip * wide_x
                new = []
                for n in range(states):
                    decay = jnp.exp2(step * decay_ref[n])
                    state = decay * held[n] + proj_ref[row * nbc + n] * driven
                    out = out + proj_ref[row * nbc + states + n] * state
                    new.append(state)
                total_ref[at, :] = total
                y_ref[at, :] = out
                return total, tuple(new)

            return lax.fori_loop(0, toks, per_tok, carried, unroll=4)

        held = tuple(start_ref[req, n] for n in range(states))
        total, held = lax.fori_loop(0, parts, per_part, (jnp.zeros((ROWS, LANES), jnp.float32), held))
        for n in range(states):
            end_ref[req, n] = held[n]
        end_ref[req, states] = total


def correct_kernel(
    place_ref, proj_ref, y_ref, total_ref, decay_ref, carry_ref, out_ref, y_scr,
):
    parts, reqs, toks, chans = out_ref.shape
    states = decay_ref.shape[0]
    rows = reqs * toks
    nbc = proj_ref.shape[0] // (parts * rows)

    def per_part(part, done):
        for req in range(reqs):
            carry = [carry_ref[req, n] for n in range(states)]

            def per_tok(tok, done, req=req, carry=carry):
                row = (part * reqs + req) * toks + tok
                at = pl.ds(pl.multiple_of(row * ROWS, ROWS), ROWS)
                total = total_ref[at, :]
                out = y_ref[at, :]
                for n in range(states):
                    out = out + proj_ref[row * nbc + states + n] * (
                        jnp.exp2(total * decay_ref[n]) * carry[n]
                    )
                y_scr[pl.ds(pl.multiple_of((req * toks + tok) * ROWS, ROWS), ROWS), :] = out
                return done

            lax.fori_loop(0, toks, per_tok, 0, unroll=4)
            tok = lax.broadcasted_iota(jnp.int32, (toks, 1), 0)
            live = place_ref[0] + part * toks + tok < place_ref[1 + req]
            for k in range(ROWS):
                block = y_scr[pl.ds(req * toks * ROWS + k, toks, stride=ROWS), :]
                out_ref[part, req, :, k * LANES : (k + 1) * LANES] = jnp.where(
                    live, block, 0.0
                ).astype(jnp.bfloat16)
        return done

    lax.fori_loop(0, parts, per_part, 0)


def shifts(count, by):
    return [(i, (i + by) % count) for i in range(count)]


def halves(array):
    top = lax.reduce_precision(array, 8, 7)
    return top.astype(jnp.bfloat16), (array - top).astype(jnp.bfloat16)


def on_device(
    conv_out, dt_low, state_proj, dt_weight, dt_bias, decay_rate, skip_gain,
    cache_states, hit_owner, hit_slot, evict_order, new_lengths,
):
    groups = lax.axis_size("cache")
    group = lax.axis_index("cache")
    hi = lax.axis_index("hi")
    lo = lax.axis_index("lo")
    reqs, toks, width = conv_out.shape
    rank = dt_low.shape[2]
    states = decay_rate.shape[0]
    nbc = state_proj.shape[2]
    slots, piece = cache_states.shape[0], cache_states.shape[3]
    chans = width // LO
    owners = hit_owner[:, 0]
    count = owners.shape[0]
    stored = cache_states.reshape(slots, states, piece)

    mine = dt_weight.shape[0] // groups
    quarter = lax.dynamic_slice_in_dim(dt_weight, group * mine, mine, 0)
    quarter = quarter.reshape(mine, HI, LO, piece).transpose(2, 0, 1, 3).reshape(LO, mine, chans)
    quarter = jnp.broadcast_to(quarter[None], (HI, LO, mine, chans)).reshape(HI * LO, mine, chans)
    quarter = lax.all_to_all(quarter, ("hi", "lo"), split_axis=0, concat_axis=0, tiled=True)
    quarter = quarter.reshape(rank // groups, chans)
    pieces = [quarter] + [
        lax.ppermute(quarter, "cache", shifts(groups, by)) for by in range(1, groups)
    ]

    slot_rows = jnp.where(owners == group, hit_slot, 0)
    picked = jnp.stack(
        [lax.dynamic_index_in_dim(stored, slot_rows[r], 0, keepdims=False) for r in range(count)]
    )
    picked = jnp.where((owners == group)[:, None, None], picked, 0).astype(jnp.bfloat16)
    picked = lax.all_to_all(picked, "cache", split_axis=0, concat_axis=0, tiled=True)
    seed = jnp.sum(
        picked.reshape(groups, reqs, states, piece).astype(jnp.float32), axis=0
    ).astype(jnp.bfloat16)
    seeds = [seed] + [lax.ppermute(seed, "hi", [(by, 0)]) for by in range(1, HI)]
    start = jnp.stack(seeds, axis=2).reshape(reqs, states, ROWS, LANES).astype(jnp.float32)
    start = jnp.where(hi == 0, start, 0.0)

    sent_x = conv_out.reshape(reqs, toks, HI, LO, piece).transpose(3, 0, 1, 2, 4)
    sent_x = sent_x.reshape(LO, reqs, toks, chans)
    dt_sorted = dt_low.reshape(reqs, toks, HI * LO, groups, mine).transpose(0, 1, 3, 2, 4)
    dt_sorted = dt_sorted.reshape(reqs, toks, rank)
    coarse, fine = halves(state_proj)
    shared = jnp.concatenate(
        [dt_sorted, coarse, fine, jnp.zeros((reqs, toks, LANES - 2 * nbc), jnp.bfloat16)], axis=2
    )
    shared = jnp.broadcast_to(shared[None], (LO,) + shared.shape)
    got = lax.all_to_all(
        jnp.concatenate([sent_x, shared], axis=3), "lo", split_axis=0, concat_axis=0, tiled=True
    )
    x_here = got[..., :chans]
    dt_here = got[..., chans : chans + rank]
    proj = got[..., chans + rank : chans + rank + nbc].astype(jnp.float32) + got[
        ..., chans + rank + nbc : chans + rank + 2 * nbc
    ].astype(jnp.float32)
    proj = proj.reshape(-1)

    weights = jnp.zeros((groups, rank // groups, chans), jnp.bfloat16)
    for by in range(groups):
        weights = lax.dynamic_update_slice_in_dim(
            weights, pieces[by][None], lax.rem(group - by + groups, groups), 0
        )
    weights = weights.reshape(rank, chans)

    def own_channels(array):
        lead = array.shape[:-1]
        array = array.reshape(lead + (HI, LO, piece))
        return lax.dynamic_index_in_dim(array, lo, len(lead) + 1, keepdims=False)

    bias = own_channels(dt_bias).reshape(1, chans)
    decay = own_channels(decay_rate).reshape(states, ROWS, LANES) * (-LOG2E)
    skip = own_channels(skip_gain).reshape(ROWS, LANES)
    lengths = lax.dynamic_slice_in_dim(new_lengths, group * reqs, reqs)
    place = jnp.concatenate([(hi * (LO * toks))[None].astype(jnp.int32), lengths])

    all_rows = LO * reqs * toks * ROWS
    smem = pl.BlockSpec(memory_space=pltpu.SMEM)
    vmem = pl.BlockSpec(memory_space=pltpu.VMEM)
    rows_f32 = jax.ShapeDtypeStruct((all_rows, LANES), jnp.float32)
    y, total, end = pl.pallas_call(
        scan_kernel,
        out_shape=(
            rows_f32,
            rows_f32,
            jax.ShapeDtypeStruct((reqs, states + 1, ROWS, LANES), jnp.float32),
        ),
        in_specs=[smem, smem] + [vmem] * 7,
        out_specs=(vmem, vmem, vmem),
        scratch_shapes=[
            pltpu.VMEM((all_rows, LANES), jnp.float32),
            pltpu.VMEM((all_rows, LANES), jnp.float32),
        ],
        compiler_params=pltpu.CompilerParams(vmem_limit_bytes=48 << 20),
        name="scan",
    )(place, proj, x_here, dt_here, weights, bias, decay, skip, start)

    end_state, end_total = end[:, :states], end[:, states:]
    total_top, total_low = halves(end_total)
    leaving = jnp.concatenate([end_state.astype(jnp.bfloat16), total_top, total_low], axis=1)
    arrived = [
        lax.ppermute(leaving, "hi", [(i, i + by) for i in range(HI - by)]) for by in range(1, HI)
    ]
    carry = jnp.zeros((reqs, states, ROWS, LANES), jnp.float32)
    for block in reversed(arrived):
        block = block.astype(jnp.float32)
        block_total = block[:, states : states + 1] + block[:, states + 1 :]
        carry = block[:, :states] + jnp.exp2(block_total * decay[None]) * carry

    out = pl.pallas_call(
        correct_kernel,
        out_shape=jax.ShapeDtypeStruct((LO, reqs, toks, chans), jnp.bfloat16),
        in_specs=[smem, smem] + [vmem] * 4,
        out_specs=vmem,
        scratch_shapes=[pltpu.VMEM((reqs * toks * ROWS, LANES), jnp.float32)],
        compiler_params=pltpu.CompilerParams(vmem_limit_bytes=48 << 20),
        name="correct",
    )(place, proj, y, total, decay, carry)

    final = (end_state + jnp.exp2(end_total * decay[None]) * carry).astype(jnp.bfloat16)
    final = final.reshape(reqs, states, HI, piece)
    held = final[:, :, HI - 1]
    for to in range(HI - 1):
        moved = lax.ppermute(final[:, :, to], "hi", [(HI - 1, to)])
        held = jnp.where(hi == to, moved, held)
    fresh = [held] + [lax.ppermute(held, "cache", shifts(groups, by)) for by in range(1, groups)]
    fresh = jnp.stack(fresh)
    source_group = lax.rem(group - jnp.arange(groups, dtype=jnp.int32) + groups, groups)
    request = (source_group[:, None] * reqs + jnp.arange(reqs, dtype=jnp.int32)[None, :]).reshape(-1)
    ids = jnp.arange(count, dtype=jnp.int32)
    ranks = jnp.sum((owners[:, None] == owners[None, :]) & (ids[None, :] < ids[:, None]), axis=1)
    target = evict_order[0][ranks]
    slot_ids = jnp.arange(slots, dtype=jnp.int32)
    fresh = fresh.reshape(count, states, piece)
    hits = (target[request][:, None] == slot_ids[None, :]) & (owners[request] == group)[:, None]
    rows = jnp.dot(
        hits.T.astype(jnp.bfloat16), fresh.reshape(count, -1), preferred_element_type=jnp.float32
    ).astype(jnp.bfloat16)
    updated = jnp.where(jnp.any(hits, axis=0)[:, None], rows, stored.reshape(slots, -1))

    back = lax.all_to_all(out, "lo", split_axis=0, concat_axis=0, tiled=True)
    back = back.reshape(LO, reqs, toks, HI, piece).transpose(1, 2, 3, 0, 4)
    return back.reshape(conv_out.shape), updated.reshape(cache_states.shape)


def solution(mesh):
    fine = Mesh(mesh.devices.reshape(mesh.shape["cache"], HI, LO, mesh.shape["head"]),
                ("cache", "hi", "lo", "head"))
    ctx = ("hi", "lo")
    in_specs = (
        P("cache", ctx, "head"),
        P("cache", ctx, None),
        P("cache", ctx, None),
        P(ctx, "head"),
        P("head"),
        P(None, "head"),
        P("head"),
        P("cache", "head", None, ctx),
        P(),
        P(),
        P("cache", None),
        P(),
    )
    out_specs = (P("cache", ctx, "head"), P("cache", "head", None, ctx))
    return jax.shard_map(
        on_device, mesh=fine, in_specs=in_specs, out_specs=out_specs, check_vma=False
    )
```

```python
import functools
import math

import jax
import jax.numpy as jnp
from jax import lax
from jax.experimental import pallas as pl
from jax.experimental.pallas import tpu as pltpu
from jax.sharding import Mesh, PartitionSpec as P

HI, LO = 4, 8
LANES, ROWS = 128, 8
LOG2E = math.log2(math.e)


def params(mib):
    return pltpu.CompilerParams(vmem_limit_bytes=mib << 20)


def cost(us):
    return pl.CostEstimate(flops=0, bytes_accessed=int(us * 3.6e6), transcendentals=0)


def spread_kernel(group_ref, w_ref, out_ref):
    width = w_ref.shape[1] // LO
    for lo in range(LO):
        block = w_ref[:, lo * width : (lo + 1) * width]
        for hi in range(HI):
            out_ref[hi * LO + lo] = block


def pack_kernel(x_ref, dt_ref, proj_ref, out_ref):
    piece = x_ref.shape[2] // (HI * LO)
    chans, rank, nbc = piece * HI, dt_ref.shape[2], proj_ref.shape[2]
    proj = proj_ref[0]
    top = proj.astype(jnp.bfloat16)
    low = (proj - top.astype(jnp.float32)).astype(jnp.bfloat16)
    pad = jnp.zeros((proj.shape[0], LANES - 2 * nbc), jnp.bfloat16)
    tail = jnp.concatenate([top, low, pad], axis=1)
    for lo in range(LO):
        for hi in range(HI):
            at = (hi * LO + lo) * piece
            out_ref[lo, :, hi * piece : (hi + 1) * piece] = x_ref[0, :, at : at + piece]
        out_ref[lo, :, chans : chans + rank] = dt_ref[0]
        out_ref[lo, :, chans + rank :] = tail


def unpack_kernel(back_ref, *refs):
    out_ref = refs[-1]
    piece = back_ref.shape[2] // HI
    for lo in range(LO):
        for hi in range(HI):
            at = (hi * LO + lo) * piece
            out_ref[0, :, at : at + piece] = back_ref[lo, :, hi * piece : (hi + 1) * piece]


def replicate(tail, first, count, scr, offset, rows, total_rows):
    depth = lax.broadcasted_iota(jnp.int32, (LANES, 2 * LANES), 0)
    side = lax.broadcasted_iota(jnp.int32, (LANES, 2 * LANES), 1) // LANES
    for n in range(0, count, 2):
        column = first + n + side
        pick = ((depth == column) | (depth == 32 + column)).astype(jnp.float32).astype(jnp.bfloat16)
        wide = jnp.dot(tail, pick, preferred_element_type=jnp.float32)
        scr[pl.ds(n * total_rows + offset, rows), :] = wide[:, :LANES]
        scr[pl.ds((n + 1) * total_rows + offset, rows), :] = wide[:, LANES:]


def to_rows(scr, refs, count):
    for p, ref in enumerate(refs):
        for j in range(2):
            value = ref[:, j * LANES : (j + 1) * LANES]
            scr[pl.ds(2 * p + j, count, stride=ROWS), :] = value


def scan_kernel(req, place_ref, lengths_ref, got_ref, *refs):
    w_refs, decay_refs, bias_refs, skip_refs = (refs[i * HI : (i + 1) * HI] for i in range(4))
    refs = refs[4 * HI :]
    before_refs, refs = refs[:-9], refs[-9:]
    if before_refs:
        seed_ref, leave_ref, *before_refs = before_refs[-2], before_refs[-1], *before_refs[:-2]
    y_ref, total_ref, end_ref, step_scr, x_scr, bc_scr, decay_scr, skip_scr, held_scr = refs
    parts, toks, _ = got_ref.shape
    rank, width = w_refs[0].shape
    chans = HI * width
    states = decay_refs[0].shape[0]
    rows = parts * toks
    hi, group = place_ref[0], place_ref[2]
    step_id = pl.program_id(0)

    @pl.when(step_id == 0)
    def _():
        to_rows(decay_scr, decay_refs, states)
        decay_scr[...] = decay_scr[...] * (-LOG2E)
        for p in range(HI):
            for j in range(2):
                skip_scr[2 * p + j : 2 * p + j + 1, :] = skip_refs[p][
                    :, j * LANES : (j + 1) * LANES
                ]
        held_scr[...] = jnp.zeros_like(held_scr)

    wide_x = got_ref[:, :, :chans].reshape(rows, chans).astype(jnp.float32)
    dt = got_ref[:, :, chans : chans + rank].reshape(rows, rank)
    tail = got_ref[:, :, chans + rank :].reshape(rows, LANES)
    position = (hi * pl.num_programs(0) + step_id) * rows + lax.broadcasted_iota(
        jnp.int32, (rows, 1), 0
    )
    live = position < lengths_ref[group * 2 + req]
    for by in range(HI):
        block = lax.rem(group - by + HI, HI)
        bias = bias_refs[0][...]
        for p in range(1, HI):
            bias = jnp.where(block == p, bias_refs[p][...], bias)
        pre = jnp.dot(dt, w_refs[by][...], preferred_element_type=jnp.float32) + bias
        step = jnp.maximum(pre, 0.0) + jnp.log1p(jnp.exp(-jnp.abs(pre)))
        step = jnp.where(live, step, 0.0)
        for j in range(2):
            step_scr[pl.ds(2 * block + j, rows, stride=ROWS), :] = step[
                :, j * LANES : (j + 1) * LANES
            ]
    for k in range(ROWS):
        x_scr[pl.ds(k, rows, stride=ROWS), :] = wide_x[:, k * LANES : (k + 1) * LANES]
    replicate(tail, 0, 2 * states, bc_scr, 0, rows, rows)
    skip = skip_scr[...]

    def per_tok(tok, carried):
        total, held = carried
        at = pl.ds(pl.multiple_of(tok * ROWS, ROWS), ROWS)
        step = step_scr[at, :]
        wide_x = x_scr[at, :]
        driven = step * wide_x
        total = total + step
        out = skip * wide_x
        new = []
        for n in range(states):
            enter = bc_scr[pl.ds(n * rows + tok, 1), :]
            leave = bc_scr[pl.ds((states + n) * rows + tok, 1), :]
            state = jnp.exp2(step * decay_scr[n * ROWS : (n + 1) * ROWS, :]) * held[n]
            state = state + enter * driven
            out = out + leave * state
            new.append(state)
        total_ref[at, :] = total
        y_ref[at, :] = out
        return total, tuple(new)

    held = tuple(held_scr[n * ROWS : (n + 1) * ROWS, :] for n in range(states))
    total, held = lax.fori_loop(
        0, rows, per_tok, (held_scr[states * ROWS :, :], held), unroll=8
    )
    for n in range(states):
        held_scr[n * ROWS : (n + 1) * ROWS, :] = held[n]
    held_scr[states * ROWS :, :] = total

    @pl.when(step_id == pl.num_programs(0) - 1)
    def _():
        end_ref[...] = held_scr[...]
        if before_refs:
            leave_ref[...] = sent_rows(list(before_refs) + [held_scr], seed_ref)


def sent_rows(ends, seed_ref):
    blocks = []
    for ref in ends:
        end = ref[...]
        total = end[-ROWS:]
        top = total.astype(jnp.bfloat16).astype(jnp.float32)
        blocks += [end[:-ROWS], top, total - top]
    for req in range(len(ends)):
        for j in range(2):
            blocks.append(seed_ref[req, :, j * LANES : (j + 1) * LANES].astype(jnp.float32))
    return jnp.concatenate(blocks, axis=0).astype(jnp.bfloat16)


def join_kernel(place_ref, *refs):
    own_ref, arrived_refs, refs = refs[0], refs[1:HI], refs[HI:]
    reqs = len(refs) - 3 - 2 * HI
    end_refs, refs = refs[:reqs], refs[reqs:]
    decay_refs, carry_ref, final_refs = refs[:HI], refs[HI], refs[HI + 1 : 2 * HI + 1]
    decay_scr, state_scr = refs[2 * HI + 1 :]
    states = decay_refs[0].shape[0]
    hi = place_ref[0]
    to_rows(decay_scr, decay_refs, states)
    per_req = (states + 2) * ROWS
    blocks = [ref[...].astype(jnp.float32) for ref in (own_ref, *arrived_refs)]
    for req in range(reqs):
        for by, block in enumerate(blocks):
            slot = lax.rem(hi - by + HI, HI)
            for j in range(2):
                at = reqs * per_req + (2 * req + j) * states
                state_scr[pl.ds(2 * slot + j, states, stride=ROWS), :] = block[at : at + states]
        for n in range(states):
            rows = slice(n * ROWS, (n + 1) * ROWS)
            decay = decay_scr[rows, :] * (-LOG2E)
            carry = state_scr[rows, :]
            for by in range(HI - 1, 0, -1):
                block = blocks[by][req * per_req : (req + 1) * per_req]
                total = block[states * ROWS : (states + 1) * ROWS] + block[(states + 1) * ROWS :]
                longer = block[rows] + jnp.exp2(total * decay) * carry
                carry = jnp.where(hi >= by, longer, carry)
            carry_ref[req, n] = carry
            total = end_refs[req][states * ROWS :, :]
            state_scr[rows, :] = end_refs[req][rows, :] + jnp.exp2(total * decay) * carry
        for p in range(HI):
            for j in range(2):
                value = state_scr[pl.ds(2 * p + j, states, stride=ROWS), :]
                final_refs[p][req, :, j * LANES : (j + 1) * LANES] = value.astype(jnp.bfloat16)


def correct_kernel(req, place_ref, lengths_ref, tail_ref, y_ref, total_ref, carry_ref, *refs):
    decay_refs, (out_ref, y_scr, c_scr, decay_scr) = refs[:HI], refs[HI:]
    parts, toks, _ = out_ref.shape
    states = decay_refs[0].shape[0]
    rows = parts * toks
    step_id = pl.program_id(0)

    @pl.when(step_id == 0)
    def _():
        to_rows(decay_scr, decay_refs, states)
        decay_scr[...] = decay_scr[...] * (-LOG2E)

    replicate(tail_ref[...].reshape(rows, LANES), states, states, c_scr, 0, rows, rows)
    carry = tuple(carry_ref[0, n] for n in range(states))

    def per_tok(tok, carry):
        at = pl.ds(pl.multiple_of(tok * ROWS, ROWS), ROWS)
        total = total_ref[at, :]
        out = y_ref[at, :]
        for n in range(states):
            leave = c_scr[pl.ds(n * rows + tok, 1), :]
            decay = decay_scr[n * ROWS : (n + 1) * ROWS, :]
            out = out + leave * (jnp.exp2(total * decay) * carry[n])
        y_scr[at, :] = out
        return carry

    lax.fori_loop(0, rows, per_tok, carry, unroll=8)
    position = (place_ref[0] * pl.num_programs(0) + step_id) * rows + lax.broadcasted_iota(
        jnp.int32, (rows, 1), 0
    )
    live = position < lengths_ref[place_ref[2] * 2 + req]
    for k in range(ROWS):
        block = jnp.where(live, y_scr[pl.ds(k, rows, stride=ROWS), :], 0.0)
        out_ref[:, :, k * LANES : (k + 1) * LANES] = block.astype(jnp.bfloat16).reshape(
            parts, toks, LANES
        )


def shifts(count, by):
    return [(i, (i + by) % count) for i in range(count)]


def on_device(
    conv_out, dt_low, state_proj, dt_weight, dt_bias, decay_rate, skip_gain,
    cache_states, hit_owner, hit_slot, evict_order, new_lengths,
):
    groups = lax.axis_size("cache")
    group = lax.axis_index("cache")
    hi = lax.axis_index("hi")
    lo = lax.axis_index("lo")
    reqs, toks, width = conv_out.shape
    rank = dt_low.shape[2]
    states = decay_rate.shape[0]
    slots, piece = cache_states.shape[0], cache_states.shape[3]
    chans = width // LO
    length = LO * toks
    owners = hit_owner[:, 0]
    count = owners.shape[0]
    sent_width = chans + rank + LANES

    def exchange(array, axis):
        return lax.all_to_all(array, axis, split_axis=0, concat_axis=0, tiled=True)

    mine = dt_weight.shape[0]
    quarter = pl.pallas_call(
        spread_kernel,
        grid_spec=pltpu.PrefetchScalarGridSpec(
            num_scalar_prefetch=1,
            grid=(1,),
            in_specs=[pl.BlockSpec((mine, width // groups), lambda i, at: (0, at[0]))],
            out_specs=pl.BlockSpec((HI * LO, mine, piece), lambda i, at: (0, 0, 0)),
        ),
        out_shape=jax.ShapeDtypeStruct((HI * LO, mine, piece), jnp.bfloat16),
        compiler_params=params(60),
        name="spread",
    )(group[None].astype(jnp.int32), dt_weight)
    quarter = exchange(quarter, ("hi", "lo")).reshape(rank, piece)

    stored = cache_states.reshape(slots, -1)
    slot_ids = jnp.arange(slots, dtype=jnp.int32)
    wanted = (hit_slot[:, None] == slot_ids[None, :]) & (owners == group)[:, None]
    picked = jnp.dot(
        wanted.astype(jnp.bfloat16), stored, preferred_element_type=jnp.float32
    ).astype(jnp.bfloat16)
    picked = picked.reshape(groups, reqs, states, piece)
    seed = lax.dynamic_index_in_dim(picked, group, 0, keepdims=False).astype(jnp.float32)
    for by in range(1, groups):
        leaving = lax.dynamic_index_in_dim(picked, lax.rem(group + by, groups), 0, keepdims=False)
        seed = seed + lax.ppermute(leaving, "cache", shifts(groups, by)).astype(jnp.float32)
    seed = seed.astype(jnp.bfloat16)

    sent = [
        pl.pallas_call(
            pack_kernel,
            grid=(1,),
            in_specs=[
                pl.BlockSpec((1, toks, n), lambda i, req=req: (req, 0, 0))
                for n in (width, rank, state_proj.shape[2])
            ],
            out_specs=pl.BlockSpec((LO, toks, sent_width), lambda i: (0, 0, 0)),
            out_shape=jax.ShapeDtypeStruct((LO, toks, sent_width), jnp.bfloat16),
            compiler_params=params(60),
            name="pack",
        )(conv_out, dt_low, state_proj)
        for req in range(reqs)
    ]
    first_sent, seed = lax.optimization_barrier((sent[0], seed))
    pieces = [quarter] + [
        lax.ppermute(quarter, "cache", shifts(groups, by)) for by in range(1, groups)
    ]
    got = [exchange(first_sent, "lo")]
    for req in range(1, reqs):
        next_sent, got[-1], pieces = lax.optimization_barrier((sent[req], got[-1], pieces))
        got.append(exchange(next_sent, "lo"))

    place = jnp.stack([hi, lo, group]).astype(jnp.int32)
    steps = 4
    parts = LO // steps
    rows = parts * toks
    rows_f32 = jax.ShapeDtypeStruct((length * ROWS, LANES), jnp.float32)
    rows_spec = pl.BlockSpec((rows * ROWS, LANES), lambda i, *at: (i, 0))
    bias, skip = dt_bias.reshape(1, width), skip_gain.reshape(1, width)

    def whole(*shape):
        return pl.BlockSpec(shape, lambda i, *at: (0,) * len(shape))

    def own(lead):
        return [
            pl.BlockSpec((lead, piece), lambda i, at, *_, p=p: (0, p * LO + at[1]))
            for p in range(HI)
        ]

    def scratch(*lengths):
        return [pltpu.VMEM((n, LANES), jnp.float32) for n in lengths]

    end_rows = (states + 1) * ROWS
    leave_rows = reqs * ((states + 2) * ROWS + 2 * states)
    y, total, end = [], [], []
    for req in range(reqs):
        last = req == reqs - 1
        one_y, one_total, one_end, *leaving = pl.pallas_call(
            functools.partial(scan_kernel, req),
            grid_spec=pltpu.PrefetchScalarGridSpec(
                num_scalar_prefetch=2,
                grid=(steps,),
                in_specs=[pl.BlockSpec((parts, toks, sent_width), lambda i, *at: (i, 0, 0))]
                + [whole(rank, piece)] * HI
                + own(states)
                + own(1) * 2
                + ([whole(end_rows, LANES)] * req + [whole(reqs, states, piece)] if last else []),
                out_specs=([whole(leave_rows, LANES)] if last else [])
                + [rows_spec, rows_spec, whole(end_rows, LANES)],
                scratch_shapes=scratch(
                    rows * ROWS, rows * ROWS, 2 * states * rows, states * ROWS, ROWS, end_rows
                ),
            ),
            out_shape=(
                [jax.ShapeDtypeStruct((leave_rows, LANES), jnp.bfloat16)] if last else []
            )
            + [rows_f32, rows_f32, jax.ShapeDtypeStruct((end_rows, LANES), jnp.float32)],
            compiler_params=params(60),
            cost_estimate=cost(15),
            name="scan",
        )(
            place, new_lengths, got[req], *pieces, *[decay_rate] * HI, *[bias] * HI,
            *[skip] * HI, *(end + [seed] if last else []),
        )
        if last:
            leaving, one_y, one_total, one_end = one_y, one_total, one_end, leaving[0]
        y.append(one_y)
        total.append(one_total)
        end.append(one_end)

    arrived = [lax.ppermute(leaving, "hi", shifts(HI, by)) for by in range(1, HI)]
    carry, *finals = pl.pallas_call(
        join_kernel,
        grid_spec=pltpu.PrefetchScalarGridSpec(
            num_scalar_prefetch=1,
            grid=(1,),
            in_specs=[whole(leave_rows, LANES)] * HI + [whole(end_rows, LANES)] * reqs + own(states),
            out_specs=[whole(reqs, states, ROWS, LANES)] + [whole(reqs, states, piece)] * HI,
            scratch_shapes=scratch(states * ROWS, states * ROWS),
        ),
        out_shape=[jax.ShapeDtypeStruct((reqs, states, ROWS, LANES), jnp.float32)]
        + [jax.ShapeDtypeStruct((reqs, states, piece), jnp.bfloat16)] * HI,
        compiler_params=params(60),
        name="join",
    )(place, leaving, *arrived, *end, *[decay_rate] * HI)

    back = []
    for req in range(reqs):
        out = pl.pallas_call(
            functools.partial(correct_kernel, req),
            grid_spec=pltpu.PrefetchScalarGridSpec(
                num_scalar_prefetch=2,
                grid=(steps,),
                in_specs=[
                    pl.BlockSpec(
                        (parts, toks, LANES), lambda i, *at: (i, 0, sent_width // LANES - 1)
                    ),
                    rows_spec,
                    rows_spec,
                    pl.BlockSpec((1, states, ROWS, LANES), lambda i, *at, req=req: (req, 0, 0, 0)),
                ]
                + own(states),
                out_specs=pl.BlockSpec((parts, toks, chans), lambda i, *at: (i, 0, 0)),
                scratch_shapes=scratch(rows * ROWS, states * rows, states * ROWS),
            ),
            out_shape=jax.ShapeDtypeStruct((LO, toks, chans), jnp.bfloat16),
            compiler_params=params(60),
            cost_estimate=cost(9),
            name="correct",
        )(place, new_lengths, got[req], y[req], total[req], carry, *[decay_rate] * HI)
        if req == reqs - 1:
            held = finals[HI - 1]
            for to in range(HI - 1):
                moved = lax.ppermute(finals[to], "hi", [(HI - 1, to)])
                held = jnp.where(hi == to, moved, held)
            out, held = lax.optimization_barrier((out, held))
        back.append(exchange(out, "lo"))

    fresh = [held] + [lax.ppermute(held, "cache", shifts(groups, by)) for by in range(1, groups)]
    fresh = jnp.stack(fresh).reshape(count, -1)
    source_group = lax.rem(group - jnp.arange(groups, dtype=jnp.int32) + groups, groups)
    request = (source_group[:, None] * reqs + jnp.arange(reqs, dtype=jnp.int32)[None, :]).reshape(-1)
    ids = jnp.arange(count, dtype=jnp.int32)
    ranks = jnp.sum((owners[:, None] == owners[None, :]) & (ids[None, :] < ids[:, None]), axis=1)
    target = evict_order[0][ranks]
    hits = (target[request][:, None] == slot_ids[None, :]) & (owners[request] == group)[:, None]
    rows = jnp.dot(
        hits.T.astype(jnp.bfloat16), fresh, preferred_element_type=jnp.float32
    ).astype(jnp.bfloat16)
    updated = jnp.where(jnp.any(hits, axis=0)[:, None], rows, stored)

    mixed = None
    for req in range(reqs):
        mixed = pl.pallas_call(
            unpack_kernel,
            grid=(1,),
            out_shape=jax.ShapeDtypeStruct(conv_out.shape, jnp.bfloat16),
            in_specs=[pl.BlockSpec((LO, toks, chans), lambda i: (0, 0, 0))]
            + ([] if mixed is None else [pl.BlockSpec(memory_space=pl.ANY)]),
            out_specs=pl.BlockSpec((1, toks, width), lambda i, req=req: (req, 0, 0)),
            input_output_aliases={} if mixed is None else {1: 0},
            compiler_params=params(16),
            name="unpack",
        )(*([back[req]] if mixed is None else [back[req], mixed]))
    return mixed, updated.reshape(cache_states.shape)


def solution(mesh):
    fine = Mesh(mesh.devices.reshape(mesh.shape["cache"], HI, LO, mesh.shape["head"]),
                ("cache", "hi", "lo", "head"))
    ctx = ("hi", "lo")
    in_specs = (
        P("cache", ctx, "head"),
        P("cache", ctx, None),
        P("cache", ctx, None),
        P(ctx, "head"),
        P("head"),
        P(None, "head"),
        P("head"),
        P("cache", "head", None, ctx),
        P(),
        P(),
        P("cache", None),
        P(),
    )
    out_specs = (P("cache", ctx, "head"), P("cache", "head", None, ctx))
    return jax.shard_map(
        on_device, mesh=fine, in_specs=in_specs, out_specs=out_specs, check_vma=False
    )
```

```python
import functools
import math

import jax
import jax.numpy as jnp
from jax import lax
from jax.experimental import pallas as pl
from jax.experimental.pallas import tpu as pltpu
from jax.sharding import Mesh, PartitionSpec as P

HI, LO = 4, 8
LANES, ROWS = 128, 8
LOG2E = math.log2(math.e)


def params(mib):
    return pltpu.CompilerParams(vmem_limit_bytes=mib << 20)


def cost(us):
    return pl.CostEstimate(flops=0, bytes_accessed=int(us * 3.6e6), transcendentals=0)


def spread_kernel(place_ref, w_ref, out_ref):
    width = w_ref.shape[1] // LO
    for lo in range(LO):
        block = w_ref[:, lo * width : (lo + 1) * width]
        for hi in range(HI):
            out_ref[hi * LO + lo] = block


def pack_kernel(place_ref, x_ref, *refs):
    out_ref = refs[-1]
    piece = x_ref.shape[2] // (HI * LO)
    for lo in range(LO):
        for hi in range(HI):
            at = (hi * LO + lo) * piece
            out_ref[lo, :, hi * piece : (hi + 1) * piece] = x_ref[0, :, at : at + piece]
        for ref in refs[:-1]:
            out_ref[lo, :, HI * piece :] = ref[...]


def unpack_kernel(place_ref, back_ref, *refs):
    out_ref = refs[-1]
    piece = back_ref.shape[2] // HI
    for lo in range(LO):
        for hi in range(HI):
            at = (hi * LO + lo) * piece
            out_ref[0, :, at : at + piece] = back_ref[lo, :, hi * piece : (hi + 1) * piece]


def replicate(tail, first, count, scr, offset, rows, total_rows):
    depth = lax.broadcasted_iota(jnp.int32, (LANES, 2 * LANES), 0)
    side = lax.broadcasted_iota(jnp.int32, (LANES, 2 * LANES), 1) // LANES
    for n in range(0, count, 2):
        column = first + n + side
        pick = ((depth == column) | (depth == 32 + column)).astype(jnp.float32).astype(jnp.bfloat16)
        wide = jnp.dot(tail, pick, preferred_element_type=jnp.float32)
        scr[pl.ds(n * total_rows + offset, rows), :] = wide[:, :LANES]
        scr[pl.ds((n + 1) * total_rows + offset, rows), :] = wide[:, LANES:]


def request_of(place_ref, turn, group):
    return group * 2 + lax.rem(place_ref[3] + turn, 2)


def to_rows(scr, refs, count):
    for p, ref in enumerate(refs):
        for j in range(2):
            value = ref[:, j * LANES : (j + 1) * LANES]
            scr[pl.ds(2 * p + j, count, stride=ROWS), :] = value


def scan_kernel(turn, place_ref, lengths_ref, got_ref, *refs):
    share_ref, refs = (got_ref, refs) if turn == 0 else (refs[0], refs[1:])
    w_refs, decay_refs, bias_refs, skip_refs = (refs[i * HI : (i + 1) * HI] for i in range(4))
    refs = refs[4 * HI :]
    before_refs, refs = refs[:-9], refs[-9:]
    if before_refs:
        leave_ref, seed_refs = before_refs[-1], before_refs[-1 - HI : -1]
        before_refs = before_refs[: -1 - HI]
    y_ref, total_ref, end_ref, step_scr, x_scr, bc_scr, decay_scr, skip_scr, held_scr = refs
    parts, toks, _ = got_ref.shape
    rank, width = w_refs[0].shape
    chans = HI * width
    states = decay_refs[0].shape[0]
    rows = parts * toks
    hi, group = place_ref[0], place_ref[2]
    step_id = pl.program_id(0)

    @pl.when(step_id == 0)
    def _():
        to_rows(decay_scr, decay_refs, states)
        decay_scr[...] = decay_scr[...] * (-LOG2E)
        for p in range(HI):
            for j in range(2):
                skip_scr[2 * p + j : 2 * p + j + 1, :] = skip_refs[p][
                    :, j * LANES : (j + 1) * LANES
                ]
        held_scr[...] = jnp.zeros_like(held_scr)

    first = chans if turn == 0 else 0
    wide_x = got_ref[:, :, :chans].reshape(rows, chans).astype(jnp.float32)
    dt = share_ref[:, :, first : first + rank].reshape(rows, rank)
    tail = share_ref[:, :, first + rank :].reshape(rows, LANES)
    position = (hi * pl.num_programs(0) + step_id) * rows + lax.broadcasted_iota(
        jnp.int32, (rows, 1), 0
    )
    live = position < lengths_ref[request_of(place_ref, turn, group)]
    for by in range(HI):
        block = lax.rem(group - by + HI, HI)
        bias = bias_refs[0][...]
        for p in range(1, HI):
            bias = jnp.where(block == p, bias_refs[p][...], bias)
        pre = jnp.dot(dt, w_refs[by][...], preferred_element_type=jnp.float32) + bias
        step = jnp.maximum(pre, 0.0) + jnp.log1p(jnp.exp(-jnp.abs(pre)))
        step = jnp.where(live, step, 0.0)
        for j in range(2):
            step_scr[pl.ds(2 * block + j, rows, stride=ROWS), :] = step[
                :, j * LANES : (j + 1) * LANES
            ]
    for k in range(ROWS):
        x_scr[pl.ds(k, rows, stride=ROWS), :] = wide_x[:, k * LANES : (k + 1) * LANES]
    replicate(tail, 0, 2 * states, bc_scr, 0, rows, rows)
    skip = skip_scr[...]

    def per_tok(tok, carried):
        total, held = carried
        at = pl.ds(pl.multiple_of(tok * ROWS, ROWS), ROWS)
        step = step_scr[at, :]
        wide_x = x_scr[at, :]
        driven = step * wide_x
        total = total + step
        out = skip * wide_x
        new = []
        for n in range(states):
            enter = bc_scr[pl.ds(n * rows + tok, 1), :]
            leave = bc_scr[pl.ds((states + n) * rows + tok, 1), :]
            state = jnp.exp2(step * decay_scr[n * ROWS : (n + 1) * ROWS, :]) * held[n]
            state = state + enter * driven
            out = out + leave * state
            new.append(state)
        total_ref[at, :] = total
        y_ref[at, :] = out
        return total, tuple(new)

    held = tuple(held_scr[n * ROWS : (n + 1) * ROWS, :] for n in range(states))
    total, held = lax.fori_loop(
        0, rows, per_tok, (held_scr[states * ROWS :, :], held), unroll=16
    )
    for n in range(states):
        held_scr[n * ROWS : (n + 1) * ROWS, :] = held[n]
    held_scr[states * ROWS :, :] = total

    @pl.when(step_id == pl.num_programs(0) - 1)
    def _():
        end_ref[...] = held_scr[...]
        if before_refs:
            leave_ref[...] = sent_rows(
                place_ref, list(before_refs) + [held_scr], seed_refs
            )


def sent_rows(place_ref, ends, seed_refs):
    blocks = []
    for ref in ends:
        end = ref[...]
        total = end[-ROWS:]
        top = total.astype(jnp.bfloat16).astype(jnp.float32)
        blocks += [end[:-ROWS], top, total - top]
    seed = sum(ref[...].astype(jnp.float32) for ref in seed_refs)
    states = seed.shape[0] // len(ends)
    seeds = [seed[req * states : (req + 1) * states] for req in range(len(ends))]
    for turn in range(len(ends)):
        mine = jnp.where(request_of(place_ref, turn, 0) == 0, seeds[0], seeds[1])
        for j in range(2):
            blocks.append(mine[:, j * LANES : (j + 1) * LANES])
    return jnp.concatenate(blocks, axis=0).astype(jnp.bfloat16)


def join_kernel(place_ref, *refs):
    own_ref, arrived_refs, refs = refs[0], refs[1:HI], refs[HI:]
    reqs = len(refs) - 3 - 2 * HI
    end_refs, refs = refs[:reqs], refs[reqs:]
    decay_refs, carry_ref, final_refs = refs[:HI], refs[HI], refs[HI + 1 : 2 * HI + 1]
    decay_scr, state_scr = refs[2 * HI + 1 :]
    states = decay_refs[0].shape[0]
    hi = place_ref[0]
    to_rows(decay_scr, decay_refs, states)
    per_req = (states + 2) * ROWS
    blocks = [ref[...].astype(jnp.float32) for ref in (own_ref, *arrived_refs)]
    for req in range(reqs):
        for by, block in enumerate(blocks):
            slot = lax.rem(hi - by + HI, HI)
            for j in range(2):
                at = reqs * per_req + (2 * req + j) * states
                state_scr[pl.ds(2 * slot + j, states, stride=ROWS), :] = block[at : at + states]
        for n in range(states):
            rows = slice(n * ROWS, (n + 1) * ROWS)
            decay = decay_scr[rows, :] * (-LOG2E)
            carry = state_scr[rows, :]
            for by in range(HI - 1, 0, -1):
                block = blocks[by][req * per_req : (req + 1) * per_req]
                total = block[states * ROWS : (states + 1) * ROWS] + block[(states + 1) * ROWS :]
                longer = block[rows] + jnp.exp2(total * decay) * carry
                carry = jnp.where(hi >= by, longer, carry)
            carry_ref[req, n] = carry
            total = end_refs[req][states * ROWS :, :]
            state_scr[rows, :] = end_refs[req][rows, :] + jnp.exp2(total * decay) * carry
        for p in range(HI):
            for j in range(2):
                value = state_scr[pl.ds(2 * p + j, states, stride=ROWS), :]
                final_refs[p][req, :, j * LANES : (j + 1) * LANES] = value.astype(jnp.bfloat16)


def correct_kernel(turn, place_ref, lengths_ref, y_ref, total_ref, carry_ref, *refs):
    decay_refs, (tail_ref, out_ref, y_scr, c_scr, decay_scr) = refs[:HI], refs[HI:]
    parts, toks, _ = out_ref.shape
    states = decay_refs[0].shape[0]
    rows = parts * toks
    step_id = pl.program_id(0)

    @pl.when(step_id == 0)
    def _():
        to_rows(decay_scr, decay_refs, states)
        decay_scr[...] = decay_scr[...] * (-LOG2E)

    replicate(tail_ref[...].reshape(rows, LANES), states, states, c_scr, 0, rows, rows)
    carry = tuple(carry_ref[0, n] for n in range(states))

    def per_tok(tok, carry):
        at = pl.ds(pl.multiple_of(tok * ROWS, ROWS), ROWS)
        total = total_ref[at, :]
        out = y_ref[at, :]
        for n in range(states):
            leave = c_scr[pl.ds(n * rows + tok, 1), :]
            decay = decay_scr[n * ROWS : (n + 1) * ROWS, :]
            out = out + leave * (jnp.exp2(total * decay) * carry[n])
        y_scr[at, :] = out
        return carry

    lax.fori_loop(0, rows, per_tok, carry, unroll=16)
    position = (place_ref[0] * pl.num_programs(0) + step_id) * rows + lax.broadcasted_iota(
        jnp.int32, (rows, 1), 0
    )
    live = position < lengths_ref[request_of(place_ref, turn, place_ref[2])]
    for k in range(ROWS):
        block = jnp.where(live, y_scr[pl.ds(k, rows, stride=ROWS), :], 0.0)
        out_ref[:, :, k * LANES : (k + 1) * LANES] = block.astype(jnp.bfloat16).reshape(
            parts, toks, LANES
        )


def shifts(count, by):
    return [(i, (i + by) % count) for i in range(count)]


def on_device(
    conv_out, dt_low, state_proj, dt_weight, dt_bias, decay_rate, skip_gain,
    cache_states, hit_owner, hit_slot, evict_order, new_lengths,
):
    groups = lax.axis_size("cache")
    group = lax.axis_index("cache")
    hi = lax.axis_index("hi")
    lo = lax.axis_index("lo")
    reqs, toks, width = conv_out.shape
    rank = dt_low.shape[2]
    states = decay_rate.shape[0]
    slots, piece = cache_states.shape[0], cache_states.shape[3]
    chans = width // LO
    length = LO * toks
    place = jnp.stack([hi, lo, group, lax.axis_index("head")]).astype(jnp.int32)
    owners = hit_owner[:, 0]
    count = owners.shape[0]
    share_width = rank + LANES

    def exchange(array, axis):
        return lax.all_to_all(array, axis, split_axis=0, concat_axis=0, tiled=True)

    mine = dt_weight.shape[0]
    quarter = pl.pallas_call(
        spread_kernel,
        grid_spec=pltpu.PrefetchScalarGridSpec(
            num_scalar_prefetch=1,
            grid=(1,),
            in_specs=[pl.BlockSpec((mine, width // groups), lambda i, at: (0, at[2]))],
            out_specs=pl.BlockSpec((HI * LO, mine, piece), lambda i, at: (0, 0, 0)),
        ),
        out_shape=jax.ShapeDtypeStruct((HI * LO, mine, piece), jnp.bfloat16),
        compiler_params=params(60),
        name="spread",
    )(place, dt_weight)
    quarter = exchange(quarter, ("hi", "lo")).reshape(rank, piece)

    stored = cache_states.reshape(slots, -1)
    slot_ids = jnp.arange(slots, dtype=jnp.int32)
    wanted = (hit_slot[:, None] == slot_ids[None, :]) & (owners == group)[:, None]
    picked = jnp.dot(
        wanted.astype(jnp.bfloat16), stored, preferred_element_type=jnp.float32
    ).astype(jnp.bfloat16)
    picked = picked.reshape(groups, reqs, states, piece)
    def of_turn(turn):
        return lambda i, at, *_: (lax.rem(at[3] + turn, 2), 0, 0)

    proj = lax.dynamic_index_in_dim(state_proj, place[3], 0, keepdims=False)
    top = lax.reduce_precision(proj, 8, 7)
    share = jnp.concatenate(
        [
            lax.dynamic_index_in_dim(dt_low, place[3], 0, keepdims=False),
            top.astype(jnp.bfloat16),
            (proj - top).astype(jnp.bfloat16),
            jnp.zeros((toks, LANES - 2 * proj.shape[1]), jnp.bfloat16),
        ],
        axis=1,
    )
    sent_width = chans + share_width
    sent = [
        pl.pallas_call(
            pack_kernel,
            grid_spec=pltpu.PrefetchScalarGridSpec(
                num_scalar_prefetch=1,
                grid=(1,),
                in_specs=[pl.BlockSpec((1, toks, width), of_turn(turn))]
                + [pl.BlockSpec((toks, share_width), lambda i, at: (0, 0))] * (turn == 0),
                out_specs=pl.BlockSpec((LO, toks, columns), lambda i, at: (0, 0, 0)),
            ),
            out_shape=jax.ShapeDtypeStruct((LO, toks, columns), jnp.bfloat16),
            compiler_params=params(60),
            name="pack",
        )(place, conv_out, *[share] * (turn == 0))
        for turn, columns in enumerate((sent_width, chans))
    ]
    first_sent, picked = lax.optimization_barrier((sent[0], picked))

    def wanted_by(member):
        return lax.dynamic_index_in_dim(picked, member, 0, keepdims=False).reshape(-1, piece)

    pieces = [quarter] + [
        lax.ppermute(
            jnp.concatenate([quarter, wanted_by(lax.rem(group + by, groups))]),
            "cache",
            shifts(groups, by),
        )
        for by in range(1, groups)
    ]
    own_seed = wanted_by(group)
    first_got = exchange(first_sent, "lo")
    second_sent, first_got, pieces = lax.optimization_barrier((sent[1], first_got, pieces))
    got = [first_got, exchange(second_sent, "lo")]
    second_share = lax.ppermute(first_got[:, :, chans:], "head", [(0, 1), (1, 0)])

    steps = 4
    parts = LO // steps
    rows = parts * toks
    rows_f32 = jax.ShapeDtypeStruct((length * ROWS, LANES), jnp.float32)
    rows_spec = pl.BlockSpec((rows * ROWS, LANES), lambda i, *at: (i, 0))
    bias, skip = dt_bias.reshape(1, width), skip_gain.reshape(1, width)

    def whole(*shape):
        return pl.BlockSpec(shape, lambda i, *at: (0,) * len(shape))

    def own(lead):
        return [
            pl.BlockSpec((lead, piece), lambda i, at, *_, p=p: (0, p * LO + at[1]))
            for p in range(HI)
        ]

    def scratch(*lengths):
        return [pltpu.VMEM((n, LANES), jnp.float32) for n in lengths]

    end_rows = (states + 1) * ROWS
    leave_rows = reqs * ((states + 2) * ROWS + 2 * states)
    y, total, end = [], [], []
    for req in range(reqs):
        last = req == reqs - 1
        one_y, one_total, one_end, *leaving = pl.pallas_call(
            functools.partial(scan_kernel, req),
            grid_spec=pltpu.PrefetchScalarGridSpec(
                num_scalar_prefetch=2,
                grid=(steps,),
                in_specs=[
                    pl.BlockSpec((parts, toks, columns), lambda i, *at: (i, 0, 0))
                    for columns in ((chans, share_width) if req else (sent_width,))
                ]
                + [whole(rank, piece)] * HI
                + own(states)
                + own(1) * 2
                + ([whole(end_rows, LANES)] * req
                   + [whole(reqs * states, piece)]
                   + [pl.BlockSpec((reqs * states, piece), lambda i, *at: (rank // (reqs * states), 0))]
                   * (groups - 1)
                   if last else []),
                out_specs=([whole(leave_rows, LANES)] if last else [])
                + [rows_spec, rows_spec, whole(end_rows, LANES)],
                scratch_shapes=scratch(
                    rows * ROWS, rows * ROWS, 2 * states * rows, states * ROWS, ROWS, end_rows
                ),
            ),
            out_shape=(
                [jax.ShapeDtypeStruct((leave_rows, LANES), jnp.bfloat16)] if last else []
            )
            + [rows_f32, rows_f32, jax.ShapeDtypeStruct((end_rows, LANES), jnp.float32)],
            compiler_params=params(60),
            cost_estimate=cost(15),
            name="scan",
        )(
            place, new_lengths, got[req], *([second_share] if req else []), *pieces, *[decay_rate] * HI, *[bias] * HI,
            *[skip] * HI, *(end + [own_seed, *pieces[1:]] if last else []),
        )
        if last:
            leaving, one_y, one_total, one_end = one_y, one_total, one_end, leaving[0]
        y.append(one_y)
        total.append(one_total)
        end.append(one_end)

    arrived = [lax.ppermute(leaving, "hi", shifts(HI, by)) for by in range(1, HI)]
    carry, *finals = pl.pallas_call(
        join_kernel,
        grid_spec=pltpu.PrefetchScalarGridSpec(
            num_scalar_prefetch=1,
            grid=(1,),
            in_specs=[whole(leave_rows, LANES)] * HI + [whole(end_rows, LANES)] * reqs + own(states),
            out_specs=[whole(reqs, states, ROWS, LANES)] + [whole(reqs, states, piece)] * HI,
            scratch_shapes=scratch(states * ROWS, states * ROWS),
        ),
        out_shape=[jax.ShapeDtypeStruct((reqs, states, ROWS, LANES), jnp.float32)]
        + [jax.ShapeDtypeStruct((reqs, states, piece), jnp.bfloat16)] * HI,
        compiler_params=params(8),
        name="join",
    )(place, leaving, *arrived, *end, *[decay_rate] * HI)

    back = []
    for req in range(reqs):
        out = pl.pallas_call(
            functools.partial(correct_kernel, req),
            grid_spec=pltpu.PrefetchScalarGridSpec(
                num_scalar_prefetch=2,
                grid=(steps,),
                in_specs=[
                    rows_spec,
                    rows_spec,
                    pl.BlockSpec((1, states, ROWS, LANES), lambda i, *at, req=req: (req, 0, 0, 0)),
                ]
                + own(states)
                + [
                    pl.BlockSpec(
                        (parts, toks, LANES),
                        lambda i, *at, at_lane=rank + (0 if req else chans): (
                            i, 0, at_lane // LANES
                        ),
                    )
                ],
                out_specs=pl.BlockSpec((parts, toks, chans), lambda i, *at: (i, 0, 0)),
                scratch_shapes=scratch(rows * ROWS, states * rows, states * ROWS),
            ),
            out_shape=jax.ShapeDtypeStruct((LO, toks, chans), jnp.bfloat16),
            compiler_params=params(60),
            cost_estimate=cost(9),
            name="correct",
        )(
            place, new_lengths, y[req], total[req], carry, *[decay_rate] * HI,
            second_share if req else first_got,
        )
        if req == reqs - 1:
            held = finals[HI - 1]
            for to in range(HI - 1):
                moved = lax.ppermute(finals[to], "hi", [(HI - 1, to)])
                held = jnp.where(hi == to, moved, held)
            out, held = lax.optimization_barrier((out, held))
        back.append(exchange(out, "lo"))

    fresh = [held] + [lax.ppermute(held, "cache", shifts(groups, by)) for by in range(1, groups)]
    fresh = jnp.stack(fresh).reshape(count, -1)
    source_group = lax.rem(group - jnp.arange(groups, dtype=jnp.int32) + groups, groups)
    turns = lax.rem(jnp.arange(reqs, dtype=jnp.int32) + place[3], reqs)
    request = (source_group[:, None] * reqs + turns[None, :]).reshape(-1)
    ids = jnp.arange(count, dtype=jnp.int32)
    ranks = jnp.sum((owners[:, None] == owners[None, :]) & (ids[None, :] < ids[:, None]), axis=1)
    target = evict_order[0][ranks]
    hits = (target[request][:, None] == slot_ids[None, :]) & (owners[request] == group)[:, None]
    rows = jnp.dot(
        hits.T.astype(jnp.bfloat16), fresh, preferred_element_type=jnp.float32
    ).astype(jnp.bfloat16)
    updated = jnp.where(jnp.any(hits, axis=0)[:, None], rows, stored)

    mixed = None
    for req in range(reqs):
        mixed = pl.pallas_call(
            unpack_kernel,
            grid_spec=pltpu.PrefetchScalarGridSpec(
                num_scalar_prefetch=1,
                grid=(1,),
                in_specs=[pl.BlockSpec((LO, toks, chans), lambda i, at: (0, 0, 0))]
                + ([] if mixed is None else [pl.BlockSpec(memory_space=pl.ANY)]),
                out_specs=pl.BlockSpec((1, toks, width), of_turn(req)),
            ),
            out_shape=jax.ShapeDtypeStruct(conv_out.shape, jnp.bfloat16),
            input_output_aliases={} if mixed is None else {2: 0},
            compiler_params=params(16),
            name="unpack",
        )(place, *([back[req]] if mixed is None else [back[req], mixed]))
    return mixed, updated.reshape(cache_states.shape)


def solution(mesh):
    fine = Mesh(mesh.devices.reshape(mesh.shape["cache"], HI, LO, mesh.shape["head"]),
                ("cache", "hi", "lo", "head"))
    ctx = ("hi", "lo")
    in_specs = (
        P("cache", ctx, "head"),
        P("cache", ctx, None),
        P("cache", ctx, None),
        P(ctx, "head"),
        P("head"),
        P(None, "head"),
        P("head"),
        P("cache", "head", None, ctx),
        P(),
        P(),
        P("cache", None),
        P(),
    )
    out_specs = (P("cache", ctx, "head"), P("cache", "head", None, ctx))
    return jax.shard_map(
        on_device, mesh=fine, in_specs=in_specs, out_specs=out_specs, check_vma=False
    )
```

```python
import functools
import math

import jax
import jax.numpy as jnp
from jax import lax
from jax.experimental import pallas as pl
from jax.experimental.pallas import tpu as pltpu
from jax.sharding import Mesh, PartitionSpec as P

HI, LO = 4, 8
LANES, ROWS = 128, 8
LOG2E = math.log2(math.e)


def params(mib):
    return pltpu.CompilerParams(vmem_limit_bytes=mib << 20)


def cost(us):
    return pl.CostEstimate(flops=0, bytes_accessed=int(us * 3.6e6), transcendentals=0)


def spread_kernel(w_ref, out_ref):
    piece = w_ref.shape[1] // (HI * LO)
    first = lax.axis_index("cache") * (LO * piece)
    for lo in range(LO):
        block = w_ref[:, pl.ds(pl.multiple_of(first + lo * piece, piece), piece)]
        for hi in range(HI):
            out_ref[hi * LO + lo] = block


def pack_kernel(place_ref, x_ref, *refs):
    out_ref = refs[-1]
    piece = x_ref.shape[2] // (HI * LO)
    for lo in range(LO):
        for hi in range(HI):
            at = (hi * LO + lo) * piece
            out_ref[lo, :, hi * piece : (hi + 1) * piece] = x_ref[0, :, at : at + piece]
        for ref in refs[:-1]:
            out_ref[lo, :, HI * piece :] = ref[...]


def unpack_kernel(place_ref, back_ref, *refs):
    out_ref = refs[-1]
    piece = back_ref.shape[2] // HI
    for lo in range(LO):
        for hi in range(HI):
            at = (hi * LO + lo) * piece
            out_ref[0, :, at : at + piece] = back_ref[lo, :, hi * piece : (hi + 1) * piece]


def replicate(tail, first, count, scr, offset, rows, total_rows):
    depth = lax.broadcasted_iota(jnp.int32, (LANES, 2 * LANES), 0)
    side = lax.broadcasted_iota(jnp.int32, (LANES, 2 * LANES), 1) // LANES
    for n in range(0, count, 2):
        column = first + n + side
        pick = ((depth == column) | (depth == 32 + column)).astype(jnp.float32).astype(jnp.bfloat16)
        wide = jnp.dot(tail, pick, preferred_element_type=jnp.float32)
        scr[pl.ds(n * total_rows + offset, rows), :] = wide[:, :LANES]
        scr[pl.ds((n + 1) * total_rows + offset, rows), :] = wide[:, LANES:]


def request_of(place_ref, turn, group):
    return group * 2 + lax.rem(place_ref[3] + turn, 2)


def to_rows(scr, refs, count):
    for p, ref in enumerate(refs):
        for j in range(2):
            value = ref[:, j * LANES : (j + 1) * LANES]
            scr[pl.ds(2 * p + j, count, stride=ROWS), :] = value


def scan_kernel(turn, place_ref, lengths_ref, got_ref, *refs):
    share_ref, refs = (got_ref, refs) if turn == 0 else (refs[0], refs[1:])
    w_refs, decay_refs, bias_refs, skip_refs = (refs[i * HI : (i + 1) * HI] for i in range(4))
    refs = refs[4 * HI :]
    before_refs, refs = refs[:-9], refs[-9:]
    if before_refs:
        leave_ref, seed_refs = before_refs[-1], before_refs[-1 - HI : -1]
        before_refs = before_refs[: -1 - HI]
    y_ref, total_ref, end_ref, step_scr, x_scr, bc_scr, decay_scr, skip_scr, held_scr = refs
    parts, toks, _ = got_ref.shape
    rank, width = w_refs[0].shape
    chans = HI * width
    states = decay_refs[0].shape[0]
    rows = parts * toks
    hi, group = place_ref[0], place_ref[2]
    step_id = pl.program_id(0)

    @pl.when(step_id == 0)
    def _():
        to_rows(decay_scr, decay_refs, states)
        decay_scr[...] = decay_scr[...] * (-LOG2E)
        for p in range(HI):
            for j in range(2):
                skip_scr[2 * p + j : 2 * p + j + 1, :] = skip_refs[p][
                    :, j * LANES : (j + 1) * LANES
                ]
        held_scr[...] = jnp.zeros_like(held_scr)

    wide_x = got_ref[:, :, :chans].reshape(rows, chans).astype(jnp.float32)
    dt = share_ref[:, :, chans : chans + rank].reshape(rows, rank)
    tail = share_ref[:, :, chans + rank :].reshape(rows, LANES)
    position = (hi * pl.num_programs(0) + step_id) * rows + lax.broadcasted_iota(
        jnp.int32, (rows, 1), 0
    )
    live = position < lengths_ref[request_of(place_ref, turn, group)]
    for by in range(HI):
        block = lax.rem(group - by + HI, HI)
        bias = bias_refs[0][...]
        for p in range(1, HI):
            bias = jnp.where(block == p, bias_refs[p][...], bias)
        pre = jnp.dot(dt, w_refs[by][...], preferred_element_type=jnp.float32) + bias
        step = jnp.maximum(pre, 0.0) + jnp.log1p(jnp.exp(-jnp.abs(pre)))
        step = jnp.where(live, step, 0.0)
        for j in range(2):
            step_scr[pl.ds(2 * block + j, rows, stride=ROWS), :] = step[
                :, j * LANES : (j + 1) * LANES
            ]
    for k in range(ROWS):
        x_scr[pl.ds(k, rows, stride=ROWS), :] = wide_x[:, k * LANES : (k + 1) * LANES]
    replicate(tail, 0, 2 * states, bc_scr, 0, rows, rows)
    skip = skip_scr[...]

    def per_tok(tok, carried):
        total, held = carried
        at = pl.ds(pl.multiple_of(tok * ROWS, ROWS), ROWS)
        step = step_scr[at, :]
        wide_x = x_scr[at, :]
        driven = step * wide_x
        total = total + step
        out = skip * wide_x
        new = []
        for n in range(states):
            enter = bc_scr[pl.ds(n * rows + tok, 1), :]
            leave = bc_scr[pl.ds((states + n) * rows + tok, 1), :]
            state = jnp.exp2(step * decay_scr[n * ROWS : (n + 1) * ROWS, :]) * held[n]
            state = state + enter * driven
            out = out + leave * state
            new.append(state)
        total_ref[at, :] = total
        y_ref[at, :] = out
        return total, tuple(new)

    held = tuple(held_scr[n * ROWS : (n + 1) * ROWS, :] for n in range(states))
    total, held = lax.fori_loop(
        0, rows, per_tok, (held_scr[states * ROWS :, :], held), unroll=32
    )
    for n in range(states):
        held_scr[n * ROWS : (n + 1) * ROWS, :] = held[n]
    held_scr[states * ROWS :, :] = total

    @pl.when(step_id == pl.num_programs(0) - 1)
    def _():
        end_ref[...] = held_scr[...]
        if before_refs:
            leave_ref[...] = sent_rows(
                place_ref, list(before_refs) + [held_scr], seed_refs
            )


def sent_rows(place_ref, ends, seed_refs):
    blocks = []
    for ref in ends:
        end = ref[...]
        total = end[-ROWS:]
        top = total.astype(jnp.bfloat16).astype(jnp.float32)
        blocks += [end[:-ROWS], top, total - top]
    seed = sum(ref[...].astype(jnp.float32) for ref in seed_refs)
    states = seed.shape[0] // len(ends)
    seeds = [seed[req * states : (req + 1) * states] for req in range(len(ends))]
    for turn in range(len(ends)):
        mine = jnp.where(request_of(place_ref, turn, 0) == 0, seeds[0], seeds[1])
        for j in range(2):
            blocks.append(mine[:, j * LANES : (j + 1) * LANES])
    return jnp.concatenate(blocks, axis=0).astype(jnp.bfloat16)


def join(place_ref, sent_refs, end_refs, decay_scr, carry_refs, final_refs, state_scr):
    states = decay_scr.shape[0] // ROWS
    reqs = len(end_refs)
    hi = place_ref[0]
    per_req = (states + 2) * ROWS
    blocks = [ref[...].astype(jnp.float32) for ref in sent_refs]
    for req in range(reqs):
        for by, block in enumerate(blocks):
            slot = lax.rem(hi - by + HI, HI)
            for j in range(2):
                at = reqs * per_req + (2 * req + j) * states
                state_scr[pl.ds(2 * slot + j, states, stride=ROWS), :] = block[at : at + states]
        for n in range(states):
            rows = slice(n * ROWS, (n + 1) * ROWS)
            decay = decay_scr[rows, :]
            carry = state_scr[rows, :]
            for by in range(HI - 1, 0, -1):
                block = blocks[by][req * per_req : (req + 1) * per_req]
                total = block[states * ROWS : (states + 1) * ROWS] + block[(states + 1) * ROWS :]
                longer = block[rows] + jnp.exp2(total * decay) * carry
                carry = jnp.where(hi >= by, longer, carry)
            carry_refs[req][rows, :] = carry
            total = end_refs[req][states * ROWS :, :]
            state_scr[rows, :] = end_refs[req][rows, :] + jnp.exp2(total * decay) * carry
        for p in range(HI):
            for j in range(2):
                value = state_scr[pl.ds(2 * p + j, states, stride=ROWS), :]
                final_refs[p][req, :, j * LANES : (j + 1) * LANES] = value.astype(jnp.bfloat16)


def correct_kernel(turn, reqs, place_ref, lengths_ref, y_ref, total_ref, tail_ref, *refs):
    decay_refs, refs = refs[:HI], refs[HI:]
    y_scr, c_scr, decay_scr, carry_scr, state_scr = refs[-5:]
    if turn == 0:
        sent_refs, end_refs, refs = refs[:HI], refs[HI : HI + reqs], refs[HI + reqs :]
        out_ref, carry_refs, final_refs = refs[0], refs[1:reqs], refs[reqs : reqs + HI]
    else:
        carry_ref, out_ref = refs[:2]
    parts, toks, _ = out_ref.shape
    states = decay_refs[0].shape[0]
    rows = parts * toks
    step_id = pl.program_id(0)

    @pl.when(step_id == 0)
    def _():
        to_rows(decay_scr, decay_refs, states)
        decay_scr[...] = decay_scr[...] * (-LOG2E)
        if turn == 0:
            carries = (carry_scr, *carry_refs)
            join(place_ref, sent_refs, end_refs, decay_scr, carries, final_refs, state_scr)
        else:
            carry_scr[...] = carry_ref[...]

    replicate(tail_ref[...].reshape(rows, LANES), states, states, c_scr, 0, rows, rows)
    carry = tuple(carry_scr[n * ROWS : (n + 1) * ROWS, :] for n in range(states))

    def per_tok(tok, carry):
        at = pl.ds(pl.multiple_of(tok * ROWS, ROWS), ROWS)
        total = total_ref[at, :]
        out = y_ref[at, :]
        for n in range(states):
            leave = c_scr[pl.ds(n * rows + tok, 1), :]
            decay = decay_scr[n * ROWS : (n + 1) * ROWS, :]
            out = out + leave * (jnp.exp2(total * decay) * carry[n])
        y_scr[at, :] = out
        return carry

    lax.fori_loop(0, rows, per_tok, carry, unroll=32)
    position = (place_ref[0] * pl.num_programs(0) + step_id) * rows + lax.broadcasted_iota(
        jnp.int32, (rows, 1), 0
    )
    live = position < lengths_ref[request_of(place_ref, turn, place_ref[2])]
    for k in range(ROWS):
        block = jnp.where(live, y_scr[pl.ds(k, rows, stride=ROWS), :], 0.0)
        out_ref[:, :, k * LANES : (k + 1) * LANES] = block.astype(jnp.bfloat16).reshape(
            parts, toks, LANES
        )


def shifts(count, by):
    return [(i, (i + by) % count) for i in range(count)]


def on_device(
    conv_out, dt_low, state_proj, dt_weight, dt_bias, decay_rate, skip_gain,
    cache_states, hit_owner, hit_slot, evict_order, new_lengths,
):
    groups = lax.axis_size("cache")
    group = lax.axis_index("cache")
    hi = lax.axis_index("hi")
    lo = lax.axis_index("lo")
    reqs, toks, width = conv_out.shape
    rank = dt_low.shape[2]
    states = decay_rate.shape[0]
    slots, piece = cache_states.shape[0], cache_states.shape[3]
    chans = width // LO
    length = LO * toks
    place = jnp.stack([hi, lo, group, lax.axis_index("head")]).astype(jnp.int32)
    owners = hit_owner[:, 0]
    count = owners.shape[0]
    share_width = rank + LANES

    def exchange(array, axis):
        return lax.all_to_all(array, axis, split_axis=0, concat_axis=0, tiled=True)

    mine = dt_weight.shape[0]
    quarter = pl.pallas_call(
        spread_kernel,
        grid=(1,),
        in_specs=[pl.BlockSpec((mine, width), lambda i: (0, 0))],
        out_specs=pl.BlockSpec((HI * LO, mine, piece), lambda i: (0, 0, 0)),
        out_shape=jax.ShapeDtypeStruct((HI * LO, mine, piece), jnp.bfloat16),
        compiler_params=params(60),
        name="spread",
    )(dt_weight)
    quarter = exchange(quarter, ("hi", "lo")).reshape(rank, piece)

    stored = cache_states.reshape(slots, -1)
    slot_ids = jnp.arange(slots, dtype=jnp.int32)
    wanted = (hit_slot[:, None] == slot_ids[None, :]) & (owners == group)[:, None]
    picked = jnp.dot(
        wanted.astype(jnp.bfloat16), stored, preferred_element_type=jnp.float32
    ).astype(jnp.bfloat16)
    picked = picked.reshape(groups, reqs, states, piece)
    def of_turn(turn):
        return lambda i, at, *_: (lax.rem(at[3] + turn, 2), 0, 0)

    proj = lax.dynamic_index_in_dim(state_proj, place[3], 0, keepdims=False)
    top = lax.reduce_precision(proj, 8, 7)
    share = jnp.concatenate(
        [
            lax.dynamic_index_in_dim(dt_low, place[3], 0, keepdims=False),
            top.astype(jnp.bfloat16),
            (proj - top).astype(jnp.bfloat16),
            jnp.zeros((toks, LANES - 2 * proj.shape[1]), jnp.bfloat16),
        ],
        axis=1,
    )
    sent_width = chans + share_width
    sent = [
        pl.pallas_call(
            pack_kernel,
            grid_spec=pltpu.PrefetchScalarGridSpec(
                num_scalar_prefetch=1,
                grid=(1,),
                in_specs=[pl.BlockSpec((1, toks, width), of_turn(turn))]
                + [pl.BlockSpec((toks, share_width), lambda i, at: (0, 0))] * (turn == 0),
                out_specs=pl.BlockSpec((LO, toks, columns), lambda i, at: (0, 0, 0)),
            ),
            out_shape=jax.ShapeDtypeStruct((LO, toks, columns), jnp.bfloat16),
            compiler_params=params(60),
            name="pack",
        )(place, conv_out, *[share] * (turn == 0))
        for turn, columns in enumerate((sent_width, chans))
    ]
    first_sent, picked = lax.optimization_barrier((sent[0], picked))

    def wanted_by(member):
        return lax.dynamic_index_in_dim(picked, member, 0, keepdims=False).reshape(-1, piece)

    pieces = [quarter] + [
        lax.ppermute(
            jnp.concatenate([quarter, wanted_by(lax.rem(group + by, groups))]),
            "cache",
            shifts(groups, by),
        )
        for by in range(1, groups)
    ]
    own_seed = wanted_by(group)
    first_got = exchange(first_sent, "lo")
    second_sent, first_got, pieces = lax.optimization_barrier((sent[1], first_got, pieces))
    got = [first_got, exchange(second_sent, "lo")]
    second_share = lax.ppermute(first_got, "head", [(0, 1), (1, 0)])

    steps = 2
    parts = LO // steps
    rows = parts * toks
    rows_f32 = jax.ShapeDtypeStruct((length * ROWS, LANES), jnp.float32)
    rows_spec = pl.BlockSpec((rows * ROWS, LANES), lambda i, *at: (i, 0))
    bias, skip = dt_bias.reshape(1, width), skip_gain.reshape(1, width)

    def whole(*shape):
        return pl.BlockSpec(shape, lambda i, *at: (0,) * len(shape))

    def own(lead):
        return [
            pl.BlockSpec((lead, piece), lambda i, at, *_, p=p: (0, p * LO + at[1]))
            for p in range(HI)
        ]

    def scratch(*lengths):
        return [pltpu.VMEM((n, LANES), jnp.float32) for n in lengths]

    end_rows = (states + 1) * ROWS
    leave_rows = reqs * ((states + 2) * ROWS + 2 * states)
    y, total, end = [], [], []
    for req in range(reqs):
        last = req == reqs - 1
        one_y, one_total, one_end, *leaving = pl.pallas_call(
            functools.partial(scan_kernel, req),
            grid_spec=pltpu.PrefetchScalarGridSpec(
                num_scalar_prefetch=2,
                grid=(steps,),
                in_specs=[
                    pl.BlockSpec((parts, toks, columns), lambda i, *at: (i, 0, 0))
                    for columns in ((chans, sent_width) if req else (sent_width,))
                ]
                + [whole(rank, piece)] * HI
                + own(states)
                + own(1) * 2
                + ([whole(end_rows, LANES)] * req
                   + [whole(reqs * states, piece)]
                   + [pl.BlockSpec((reqs * states, piece), lambda i, *at: (rank // (reqs * states), 0))]
                   * (groups - 1)
                   if last else []),
                out_specs=([whole(leave_rows, LANES)] if last else [])
                + [rows_spec, rows_spec, whole(end_rows, LANES)],
                scratch_shapes=scratch(
                    rows * ROWS, rows * ROWS, 2 * states * rows, states * ROWS, ROWS, end_rows
                ),
            ),
            out_shape=(
                [jax.ShapeDtypeStruct((leave_rows, LANES), jnp.bfloat16)] if last else []
            )
            + [rows_f32, rows_f32, jax.ShapeDtypeStruct((end_rows, LANES), jnp.float32)],
            compiler_params=params(60),
            cost_estimate=cost(15),
            name="scan",
        )(
            place, new_lengths, got[req], *([second_share] if req else []), *pieces, *[decay_rate] * HI, *[bias] * HI,
            *[skip] * HI, *(end + [own_seed, *pieces[1:]] if last else []),
        )
        if last:
            leaving, one_y, one_total, one_end = one_y, one_total, one_end, leaving[0]
        y.append(one_y)
        total.append(one_total)
        end.append(one_end)

    arrived = [lax.ppermute(leaving, "hi", shifts(HI, by)) for by in range(1, HI)]
    carry_rows = states * ROWS
    back, carry = [], None
    for req in range(reqs):
        out, *more = pl.pallas_call(
            functools.partial(correct_kernel, req, reqs),
            grid_spec=pltpu.PrefetchScalarGridSpec(
                num_scalar_prefetch=2,
                grid=(steps,),
                in_specs=[
                    rows_spec,
                    rows_spec,
                    pl.BlockSpec(
                        (parts, toks, LANES), lambda i, *at: (i, 0, (chans + rank) // LANES)
                    ),
                ]
                + own(states)
                + (
                    [whole(carry_rows, LANES)]
                    if req
                    else [whole(leave_rows, LANES)] * HI + [whole(end_rows, LANES)] * reqs
                ),
                out_specs=[pl.BlockSpec((parts, toks, chans), lambda i, *at: (i, 0, 0))]
                + (
                    []
                    if req
                    else [whole(carry_rows, LANES)] * (reqs - 1)
                    + [whole(reqs, states, piece)] * HI
                ),
                scratch_shapes=scratch(
                    rows * ROWS, states * rows, carry_rows, carry_rows, carry_rows
                ),
            ),
            out_shape=[jax.ShapeDtypeStruct((LO, toks, chans), jnp.bfloat16)]
            + (
                []
                if req
                else [jax.ShapeDtypeStruct((carry_rows, LANES), jnp.float32)] * (reqs - 1)
                + [jax.ShapeDtypeStruct((reqs, states, piece), jnp.bfloat16)] * HI
            ),
            compiler_params=params(60),
            cost_estimate=cost(9),
            name="correct",
        )(
            place, new_lengths, y[req], total[req], second_share if req else first_got,
            *[decay_rate] * HI, *([carry[req - 1]] if req else [leaving, *arrived, *end]),
        )
        if req == 0:
            carry, finals = more[: reqs - 1], more[reqs - 1 :]
        if req == reqs - 1:
            held = finals[HI - 1]
            for to in range(HI - 1):
                moved = lax.ppermute(finals[to], "hi", [(HI - 1, to)])
                held = jnp.where(hi == to, moved, held)
            out, held = lax.optimization_barrier((out, held))
        back.append(exchange(out, "lo"))

    fresh = [held] + [lax.ppermute(held, "cache", shifts(groups, by)) for by in range(1, groups)]
    fresh = jnp.stack(fresh).reshape(count, -1)
    source_group = lax.rem(group - jnp.arange(groups, dtype=jnp.int32) + groups, groups)
    turns = lax.rem(jnp.arange(reqs, dtype=jnp.int32) + place[3], reqs)
    request = (source_group[:, None] * reqs + turns[None, :]).reshape(-1)
    ids = jnp.arange(count, dtype=jnp.int32)
    ranks = jnp.sum((owners[:, None] == owners[None, :]) & (ids[None, :] < ids[:, None]), axis=1)
    target = evict_order[0][ranks]
    hits = (target[request][:, None] == slot_ids[None, :]) & (owners[request] == group)[:, None]
    rows = jnp.dot(
        hits.T.astype(jnp.bfloat16), fresh, preferred_element_type=jnp.float32
    ).astype(jnp.bfloat16)
    updated = jnp.where(jnp.any(hits, axis=0)[:, None], rows, stored)

    mixed = None
    for req in range(reqs):
        mixed = pl.pallas_call(
            unpack_kernel,
            grid_spec=pltpu.PrefetchScalarGridSpec(
                num_scalar_prefetch=1,
                grid=(1,),
                in_specs=[pl.BlockSpec((LO, toks, chans), lambda i, at: (0, 0, 0))]
                + ([] if mixed is None else [pl.BlockSpec(memory_space=pl.ANY)]),
                out_specs=pl.BlockSpec((1, toks, width), of_turn(req)),
            ),
            out_shape=jax.ShapeDtypeStruct(conv_out.shape, jnp.bfloat16),
            input_output_aliases={} if mixed is None else {2: 0},
            compiler_params=params(16),
            name="unpack",
        )(place, *([back[req]] if mixed is None else [back[req], mixed]))
    return mixed, updated.reshape(cache_states.shape)


def solution(mesh):
    fine = Mesh(mesh.devices.reshape(mesh.shape["cache"], HI, LO, mesh.shape["head"]),
                ("cache", "hi", "lo", "head"))
    ctx = ("hi", "lo")
    in_specs = (
        P("cache", ctx, "head"),
        P("cache", ctx, None),
        P("cache", ctx, None),
        P(ctx, "head"),
        P("head"),
        P(None, "head"),
        P("head"),
        P("cache", "head", None, ctx),
        P(),
        P(),
        P("cache", None),
        P(),
    )
    out_specs = (P("cache", ctx, "head"), P("cache", "head", None, ctx))
    return jax.shard_map(
        on_device, mesh=fine, in_specs=in_specs, out_specs=out_specs, check_vma=False
    )
```

```python
import functools
import math

import jax
import jax.numpy as jnp
from jax import lax
from jax.experimental import pallas as pl
from jax.experimental.pallas import tpu as pltpu
from jax.sharding import Mesh, PartitionSpec as P

HI, LO = 4, 8
LANES, ROWS = 128, 8
LOG2E = math.log2(math.e)


def params(mib):
    return pltpu.CompilerParams(vmem_limit_bytes=mib << 20)


def cost(us):
    return pl.CostEstimate(flops=0, bytes_accessed=int(us * 3.6e6), transcendentals=0)


def spread_kernel(w_ref, out_ref):
    piece = w_ref.shape[1] // (HI * LO)
    first = lax.axis_index("cache") * (LO * piece)
    for lo in range(LO):
        block = w_ref[:, pl.ds(pl.multiple_of(first + lo * piece, piece), piece)]
        for hi in range(HI):
            out_ref[hi * LO + lo] = block


def pack_kernel(place_ref, x_ref, *refs):
    out_ref = refs[-1]
    piece = x_ref.shape[2] // (HI * LO)
    for lo in range(LO):
        for hi in range(HI):
            at = (hi * LO + lo) * piece
            out_ref[lo, :, hi * piece : (hi + 1) * piece] = x_ref[0, :, at : at + piece]
        for ref in refs[:-1]:
            out_ref[lo, :, HI * piece :] = ref[...]


def unpack_kernel(place_ref, back_ref, *refs):
    out_ref = refs[-1]
    piece = back_ref.shape[2] // HI
    for lo in range(LO):
        for hi in range(HI):
            at = (hi * LO + lo) * piece
            out_ref[0, :, at : at + piece] = back_ref[lo, :, hi * piece : (hi + 1) * piece]


def replicate(tail, first, count, scr, offset, rows, total_rows):
    depth = lax.broadcasted_iota(jnp.int32, (LANES, 2 * LANES), 0)
    side = lax.broadcasted_iota(jnp.int32, (LANES, 2 * LANES), 1) // LANES
    for n in range(0, count, 2):
        column = first + n + side
        pick = ((depth == column) | (depth == 32 + column)).astype(jnp.float32).astype(jnp.bfloat16)
        wide = jnp.dot(tail, pick, preferred_element_type=jnp.float32)
        scr[pl.ds(n * total_rows + offset, rows), :] = wide[:, :LANES]
        scr[pl.ds((n + 1) * total_rows + offset, rows), :] = wide[:, LANES:]


def request_of(place_ref, turn, group):
    return group * 2 + lax.rem(place_ref[3] + turn, 2)


def to_rows(scr, refs, count):
    for p, ref in enumerate(refs):
        for j in range(2):
            value = ref[:, j * LANES : (j + 1) * LANES]
            scr[pl.ds(2 * p + j, count, stride=ROWS), :] = value


def scan_kernel(turn, place_ref, lengths_ref, got_ref, *refs):
    share_ref, refs = (got_ref, refs) if turn == 0 else (refs[0], refs[1:])
    w_refs, decay_refs, bias_refs, skip_refs = (refs[i * HI : (i + 1) * HI] for i in range(4))
    refs = refs[4 * HI :]
    before_refs, refs = refs[:-9], refs[-9:]
    if before_refs:
        leave_ref, seed_refs = before_refs[-1], before_refs[-1 - HI : -1]
        before_refs = before_refs[: -1 - HI]
    y_ref, total_ref, end_ref, step_scr, x_scr, bc_scr, decay_scr, skip_scr, held_scr = refs
    parts, toks, _ = got_ref.shape
    rank, width = w_refs[0].shape
    chans = HI * width
    states = decay_refs[0].shape[0]
    rows = parts * toks
    hi, group = place_ref[0], place_ref[2]
    step_id = pl.program_id(0)

    @pl.when(step_id == 0)
    def _():
        to_rows(decay_scr, decay_refs, states)
        decay_scr[...] = decay_scr[...] * (-LOG2E)
        for p in range(HI):
            for j in range(2):
                skip_scr[2 * p + j : 2 * p + j + 1, :] = skip_refs[p][
                    :, j * LANES : (j + 1) * LANES
                ]
        held_scr[...] = jnp.zeros_like(held_scr)

    wide_x = got_ref[:, :, :chans].reshape(rows, chans).astype(jnp.float32)
    dt = share_ref[:, :, chans : chans + rank].reshape(rows, rank)
    tail = share_ref[:, :, chans + rank :].reshape(rows, LANES)
    position = (hi * pl.num_programs(0) + step_id) * rows + lax.broadcasted_iota(
        jnp.int32, (rows, 1), 0
    )
    live = position < lengths_ref[request_of(place_ref, turn, group)]
    for by in range(HI):
        block = lax.rem(group - by + HI, HI)
        bias = bias_refs[0][...]
        for p in range(1, HI):
            bias = jnp.where(block == p, bias_refs[p][...], bias)
        pre = jnp.dot(dt, w_refs[by][...], preferred_element_type=jnp.float32) + bias
        step = jnp.maximum(pre, 0.0) + jnp.log1p(jnp.exp(-jnp.abs(pre)))
        step = jnp.where(live, step, 0.0)
        for j in range(2):
            step_scr[pl.ds(2 * block + j, rows, stride=ROWS), :] = step[
                :, j * LANES : (j + 1) * LANES
            ]
    for k in range(ROWS):
        x_scr[pl.ds(k, rows, stride=ROWS), :] = wide_x[:, k * LANES : (k + 1) * LANES]
    replicate(tail, 0, 2 * states, bc_scr, 0, rows, rows)
    skip = skip_scr[...]

    def per_tok(tok, carried):
        total, held = carried
        at = pl.ds(pl.multiple_of(tok * ROWS, ROWS), ROWS)
        step = step_scr[at, :]
        wide_x = x_scr[at, :]
        driven = step * wide_x
        total = total + step
        out = skip * wide_x
        new = []
        for n in range(states):
            enter = bc_scr[pl.ds(n * rows + tok, 1), :]
            leave = bc_scr[pl.ds((states + n) * rows + tok, 1), :]
            state = jnp.exp2(step * decay_scr[n * ROWS : (n + 1) * ROWS, :]) * held[n]
            state = state + enter * driven
            out = out + leave * state
            new.append(state)
        total_ref[at, :] = total
        y_ref[at, :] = out
        return total, tuple(new)

    held = tuple(held_scr[n * ROWS : (n + 1) * ROWS, :] for n in range(states))
    total, held = lax.fori_loop(
        0, rows, per_tok, (held_scr[states * ROWS :, :], held), unroll=32
    )
    for n in range(states):
        held_scr[n * ROWS : (n + 1) * ROWS, :] = held[n]
    held_scr[states * ROWS :, :] = total

    @pl.when(step_id == pl.num_programs(0) - 1)
    def _():
        end_ref[...] = held_scr[...]
        if before_refs:
            leave_ref[...] = sent_rows(
                place_ref, list(before_refs) + [held_scr], seed_refs
            )


def sent_rows(place_ref, ends, seed_refs):
    blocks = []
    for ref in ends:
        end = ref[...]
        total = end[-ROWS:]
        top = total.astype(jnp.bfloat16).astype(jnp.float32)
        blocks += [end[:-ROWS], top, total - top]
    seed = sum(ref[...].astype(jnp.float32) for ref in seed_refs)
    states = seed.shape[0] // len(ends)
    seeds = [seed[req * states : (req + 1) * states] for req in range(len(ends))]
    for turn in range(len(ends)):
        mine = jnp.where(request_of(place_ref, turn, 0) == 0, seeds[0], seeds[1])
        for j in range(2):
            blocks.append(mine[:, j * LANES : (j + 1) * LANES])
    return jnp.concatenate(blocks, axis=0).astype(jnp.bfloat16)


def join(place_ref, sent_refs, end_refs, decay_scr, carry_refs, final_refs, state_scr):
    states = decay_scr.shape[0] // ROWS
    reqs = len(end_refs)
    hi = place_ref[0]
    per_req = (states + 2) * ROWS
    blocks = [ref[...].astype(jnp.float32) for ref in sent_refs]
    for req in range(reqs):
        for by, block in enumerate(blocks):
            slot = lax.rem(hi - by + HI, HI)
            for j in range(2):
                at = reqs * per_req + (2 * req + j) * states
                state_scr[pl.ds(2 * slot + j, states, stride=ROWS), :] = block[at : at + states]
        for n in range(states):
            rows = slice(n * ROWS, (n + 1) * ROWS)
            decay = decay_scr[rows, :]
            carry = state_scr[rows, :]
            for by in range(HI - 1, 0, -1):
                block = blocks[by][req * per_req : (req + 1) * per_req]
                total = block[states * ROWS : (states + 1) * ROWS] + block[(states + 1) * ROWS :]
                longer = block[rows] + jnp.exp2(total * decay) * carry
                carry = jnp.where(hi >= by, longer, carry)
            carry_refs[req][rows, :] = carry
            total = end_refs[req][states * ROWS :, :]
            state_scr[rows, :] = end_refs[req][rows, :] + jnp.exp2(total * decay) * carry
        for p in range(HI):
            for j in range(2):
                value = state_scr[pl.ds(2 * p + j, states, stride=ROWS), :]
                final_refs[p][req, :, j * LANES : (j + 1) * LANES] = value.astype(jnp.bfloat16)


def correct_kernel(turn, reqs, place_ref, lengths_ref, y_ref, total_ref, tail_ref, *refs):
    decay_refs, refs = refs[:HI], refs[HI:]
    y_scr, c_scr, decay_scr, carry_scr, state_scr = refs[-5:]
    if turn == 0:
        sent_refs, end_refs, refs = refs[:HI], refs[HI : HI + reqs], refs[HI + reqs :]
        out_ref, carry_refs, final_refs = refs[0], refs[1:reqs], refs[reqs : reqs + HI]
    else:
        carry_ref, out_ref = refs[:2]
    parts, toks, _ = out_ref.shape
    states = decay_refs[0].shape[0]
    rows = parts * toks
    step_id = pl.program_id(0)

    @pl.when(step_id == 0)
    def _():
        to_rows(decay_scr, decay_refs, states)
        decay_scr[...] = decay_scr[...] * (-LOG2E)
        if turn == 0:
            carries = (carry_scr, *carry_refs)
            join(place_ref, sent_refs, end_refs, decay_scr, carries, final_refs, state_scr)
        else:
            carry_scr[...] = carry_ref[...]

    replicate(tail_ref[...].reshape(rows, LANES), states, states, c_scr, 0, rows, rows)
    carry = tuple(carry_scr[n * ROWS : (n + 1) * ROWS, :] for n in range(states))

    def per_tok(tok, carry):
        at = pl.ds(pl.multiple_of(tok * ROWS, ROWS), ROWS)
        total = total_ref[at, :]
        out = y_ref[at, :]
        for n in range(states):
            leave = c_scr[pl.ds(n * rows + tok, 1), :]
            decay = decay_scr[n * ROWS : (n + 1) * ROWS, :]
            out = out + leave * (jnp.exp2(total * decay) * carry[n])
        y_scr[at, :] = out
        return carry

    lax.fori_loop(0, rows, per_tok, carry, unroll=32)
    position = (place_ref[0] * pl.num_programs(0) + step_id) * rows + lax.broadcasted_iota(
        jnp.int32, (rows, 1), 0
    )
    live = position < lengths_ref[request_of(place_ref, turn, place_ref[2])]
    for k in range(ROWS):
        block = jnp.where(live, y_scr[pl.ds(k, rows, stride=ROWS), :], 0.0)
        out_ref[:, :, k * LANES : (k + 1) * LANES] = block.astype(jnp.bfloat16).reshape(
            parts, toks, LANES
        )


def shifts(count, by):
    return [(i, (i + by) % count) for i in range(count)]


def on_device(
    conv_out, dt_low, state_proj, dt_weight, dt_bias, decay_rate, skip_gain,
    cache_states, hit_owner, hit_slot, evict_order, new_lengths,
):
    groups = lax.axis_size("cache")
    group = lax.axis_index("cache")
    hi = lax.axis_index("hi")
    lo = lax.axis_index("lo")
    reqs, toks, width = conv_out.shape
    rank = dt_low.shape[2]
    states = decay_rate.shape[0]
    slots, piece = cache_states.shape[0], cache_states.shape[3]
    chans = width // LO
    length = LO * toks
    place = jnp.stack([hi, lo, group, lax.axis_index("head")]).astype(jnp.int32)
    owners = hit_owner[:, 0]
    count = owners.shape[0]
    share_width = rank + LANES

    def exchange(array, axis):
        return lax.all_to_all(array, axis, split_axis=0, concat_axis=0, tiled=True)

    mine = dt_weight.shape[0]
    quarter = pl.pallas_call(
        spread_kernel,
        grid=(1,),
        in_specs=[pl.BlockSpec((mine, width), lambda i: (0, 0))],
        out_specs=pl.BlockSpec((HI * LO, mine, piece), lambda i: (0, 0, 0)),
        out_shape=jax.ShapeDtypeStruct((HI * LO, mine, piece), jnp.bfloat16),
        compiler_params=params(63),
        name="spread",
    )(dt_weight)
    quarter = exchange(quarter, ("hi", "lo")).reshape(rank, piece)

    stored = cache_states.reshape(slots, -1)
    slot_ids = jnp.arange(slots, dtype=jnp.int32)
    wanted = (hit_slot[:, None] == slot_ids[None, :]) & (owners == group)[:, None]
    picked = jnp.dot(
        wanted.astype(jnp.bfloat16), stored, preferred_element_type=jnp.float32
    ).astype(jnp.bfloat16)
    picked = picked.reshape(groups, reqs, states, piece)
    source_group = lax.rem(group - jnp.arange(groups, dtype=jnp.int32) + groups, groups)
    turns = lax.rem(jnp.arange(reqs, dtype=jnp.int32) + place[3], reqs)
    request = (source_group[:, None] * reqs + turns[None, :]).reshape(-1)
    ids = jnp.arange(count, dtype=jnp.int32)
    ranks = jnp.sum((owners[:, None] == owners[None, :]) & (ids[None, :] < ids[:, None]), axis=1)
    target = evict_order[0][ranks]
    hits = (target[request][:, None] == slot_ids[None, :]) & (owners[request] == group)[:, None]

    def of_turn(turn):
        return lambda i, at, *_: (lax.rem(at[3] + turn, 2), 0, 0)

    proj = lax.dynamic_index_in_dim(state_proj, place[3], 0, keepdims=False)
    top = lax.reduce_precision(proj, 8, 7)
    share = jnp.concatenate(
        [
            lax.dynamic_index_in_dim(dt_low, place[3], 0, keepdims=False),
            top.astype(jnp.bfloat16),
            (proj - top).astype(jnp.bfloat16),
            jnp.zeros((toks, LANES - 2 * proj.shape[1]), jnp.bfloat16),
        ],
        axis=1,
    )
    sent_width = chans + share_width
    sent = [
        pl.pallas_call(
            pack_kernel,
            grid_spec=pltpu.PrefetchScalarGridSpec(
                num_scalar_prefetch=1,
                grid=(1,),
                in_specs=[pl.BlockSpec((1, toks, width), of_turn(turn))]
                + [pl.BlockSpec((toks, share_width), lambda i, at: (0, 0))] * (turn == 0),
                out_specs=pl.BlockSpec((LO, toks, columns), lambda i, at: (0, 0, 0)),
            ),
            out_shape=jax.ShapeDtypeStruct((LO, toks, columns), jnp.bfloat16),
            compiler_params=params(63),
            name="pack",
        )(place, conv_out, *[share] * (turn == 0))
        for turn, columns in enumerate((sent_width, chans))
    ]
    first_sent, picked = lax.optimization_barrier((sent[0], picked))

    def wanted_by(member):
        return lax.dynamic_index_in_dim(picked, member, 0, keepdims=False).reshape(-1, piece)

    pieces = [quarter] + [
        lax.ppermute(
            jnp.concatenate([quarter, wanted_by(lax.rem(group + by, groups))]),
            "cache",
            shifts(groups, by),
        )
        for by in range(1, groups)
    ]
    own_seed = wanted_by(group)
    first_got = exchange(first_sent, "lo")
    second_sent, first_got, pieces, hits = lax.optimization_barrier(
        (sent[1], first_got, pieces, hits)
    )
    got = [first_got, exchange(second_sent, "lo")]
    second_share = lax.ppermute(first_got, "head", [(0, 1), (1, 0)])

    steps = 2
    parts = LO // steps
    rows = parts * toks
    rows_f32 = jax.ShapeDtypeStruct((length * ROWS, LANES), jnp.float32)
    rows_spec = pl.BlockSpec((rows * ROWS, LANES), lambda i, *at: (i, 0))
    bias, skip = dt_bias.reshape(1, width), skip_gain.reshape(1, width)

    def whole(*shape):
        return pl.BlockSpec(shape, lambda i, *at: (0,) * len(shape))

    def own(lead):
        return [
            pl.BlockSpec((lead, piece), lambda i, at, *_, p=p: (0, p * LO + at[1]))
            for p in range(HI)
        ]

    def scratch(*lengths):
        return [pltpu.VMEM((n, LANES), jnp.float32) for n in lengths]

    end_rows = (states + 1) * ROWS
    leave_rows = reqs * ((states + 2) * ROWS + 2 * states)
    y, total, end = [], [], []
    for req in range(reqs):
        last = req == reqs - 1
        one_y, one_total, one_end, *leaving = pl.pallas_call(
            functools.partial(scan_kernel, req),
            grid_spec=pltpu.PrefetchScalarGridSpec(
                num_scalar_prefetch=2,
                grid=(steps,),
                in_specs=[
                    pl.BlockSpec((parts, toks, columns), lambda i, *at: (i, 0, 0))
                    for columns in ((chans, sent_width) if req else (sent_width,))
                ]
                + [whole(rank, piece)] * HI
                + own(states)
                + own(1) * 2
                + ([whole(end_rows, LANES)] * req
                   + [whole(reqs * states, piece)]
                   + [pl.BlockSpec((reqs * states, piece), lambda i, *at: (rank // (reqs * states), 0))]
                   * (groups - 1)
                   if last else []),
                out_specs=([whole(leave_rows, LANES)] if last else [])
                + [rows_spec, rows_spec, whole(end_rows, LANES)],
                scratch_shapes=scratch(
                    rows * ROWS, rows * ROWS, 2 * states * rows, states * ROWS, ROWS, end_rows
                ),
            ),
            out_shape=(
                [jax.ShapeDtypeStruct((leave_rows, LANES), jnp.bfloat16)] if last else []
            )
            + [rows_f32, rows_f32, jax.ShapeDtypeStruct((end_rows, LANES), jnp.float32)],
            compiler_params=params(63),
            cost_estimate=cost(15),
            name="scan",
        )(
            place, new_lengths, got[req], *([second_share] if req else []), *pieces, *[decay_rate] * HI, *[bias] * HI,
            *[skip] * HI, *(end + [own_seed, *pieces[1:]] if last else []),
        )
        if last:
            leaving, one_y, one_total, one_end = one_y, one_total, one_end, leaving[0]
        y.append(one_y)
        total.append(one_total)
        end.append(one_end)

    arrived = [lax.ppermute(leaving, "hi", shifts(HI, by)) for by in range(1, HI)]
    carry_rows = states * ROWS
    back, carry = [], None
    for req in range(reqs):
        out, *more = pl.pallas_call(
            functools.partial(correct_kernel, req, reqs),
            grid_spec=pltpu.PrefetchScalarGridSpec(
                num_scalar_prefetch=2,
                grid=(steps,),
                in_specs=[
                    rows_spec,
                    rows_spec,
                    pl.BlockSpec(
                        (parts, toks, LANES), lambda i, *at: (i, 0, (chans + rank) // LANES)
                    ),
                ]
                + own(states)
                + (
                    [whole(carry_rows, LANES)]
                    if req
                    else [whole(leave_rows, LANES)] * HI + [whole(end_rows, LANES)] * reqs
                ),
                out_specs=[pl.BlockSpec((parts, toks, chans), lambda i, *at: (i, 0, 0))]
                + (
                    []
                    if req
                    else [whole(carry_rows, LANES)] * (reqs - 1)
                    + [whole(reqs, states, piece)] * HI
                ),
                scratch_shapes=scratch(
                    rows * ROWS, states * rows, carry_rows, carry_rows, carry_rows
                ),
            ),
            out_shape=[jax.ShapeDtypeStruct((LO, toks, chans), jnp.bfloat16)]
            + (
                []
                if req
                else [jax.ShapeDtypeStruct((carry_rows, LANES), jnp.float32)] * (reqs - 1)
                + [jax.ShapeDtypeStruct((reqs, states, piece), jnp.bfloat16)] * HI
            ),
            compiler_params=params(63),
            cost_estimate=cost(9),
            name="correct",
        )(
            place, new_lengths, y[req], total[req], second_share if req else first_got,
            *[decay_rate] * HI, *([carry[req - 1]] if req else [leaving, *arrived, *end]),
        )
        if req == 0:
            carry, finals = more[: reqs - 1], more[reqs - 1 :]
        if req == reqs - 1:
            held = finals[HI - 1]
            for to in range(HI - 1):
                moved = lax.ppermute(finals[to], "hi", [(HI - 1, to)])
                held = jnp.where(hi == to, moved, held)
            out, held = lax.optimization_barrier((out, held))
        back.append(exchange(out, "lo"))

    def unpack(turn, mixed):
        return pl.pallas_call(
            unpack_kernel,
            grid_spec=pltpu.PrefetchScalarGridSpec(
                num_scalar_prefetch=1,
                grid=(1,),
                in_specs=[whole(LO, toks, chans)]
                + [pl.BlockSpec(memory_space=pl.ANY)] * len(mixed),
                out_specs=pl.BlockSpec((1, toks, width), of_turn(turn)),
            ),
            out_shape=jax.ShapeDtypeStruct(conv_out.shape, jnp.bfloat16),
            input_output_aliases={2: 0} if mixed else {},
            compiler_params=params(16),
            name="unpack",
        )(place, back[turn], *mixed)

    mixed = unpack(0, [])
    held, mixed = lax.optimization_barrier((held, mixed))
    for turn in range(1, reqs):
        mixed = unpack(turn, [mixed])

    fresh = [held] + [lax.ppermute(held, "cache", shifts(groups, by)) for by in range(1, groups)]
    fresh = jnp.stack(fresh).reshape(count, -1)
    rows = jnp.dot(
        hits.T.astype(jnp.bfloat16), fresh, preferred_element_type=jnp.float32
    ).astype(jnp.bfloat16)
    updated = jnp.where(jnp.any(hits, axis=0)[:, None], rows, stored)

    return mixed, updated.reshape(cache_states.shape)


def solution(mesh):
    fine = Mesh(mesh.devices.reshape(mesh.shape["cache"], HI, LO, mesh.shape["head"]),
                ("cache", "hi", "lo", "head"))
    ctx = ("hi", "lo")
    in_specs = (
        P("cache", ctx, "head"),
        P("cache", ctx, None),
        P("cache", ctx, None),
        P(ctx, "head"),
        P("head"),
        P(None, "head"),
        P("head"),
        P("cache", "head", None, ctx),
        P(),
        P(),
        P("cache", None),
        P(),
    )
    out_specs = (P("cache", ctx, "head"), P("cache", "head", None, ctx))
    return jax.shard_map(
        on_device, mesh=fine, in_specs=in_specs, out_specs=out_specs, check_vma=False
    )
```

```python
import functools
import math

import jax
import jax.numpy as jnp
from jax import lax
from jax.experimental import pallas as pl
from jax.experimental.pallas import tpu as pltpu
from jax.sharding import Mesh, PartitionSpec as P

HI, LO = 4, 8
LANES, ROWS = 128, 8
LOG2E = math.log2(math.e)


def params(mib):
    return pltpu.CompilerParams(vmem_limit_bytes=mib << 20)


def cost(us):
    return pl.CostEstimate(flops=0, bytes_accessed=int(us * 3.6e6), transcendentals=0)


def spread_kernel(w_ref, out_ref):
    piece = w_ref.shape[1] // (HI * LO)
    first = lax.axis_index("cache") * (LO * piece)
    for lo in range(LO):
        block = w_ref[:, pl.ds(pl.multiple_of(first + lo * piece, piece), piece)]
        for hi in range(HI):
            out_ref[hi * LO + lo] = block


def pack_kernel(place_ref, x_ref, *refs):
    out_ref = refs[-1]
    piece = x_ref.shape[2] // (HI * LO)
    for lo in range(LO):
        for hi in range(HI):
            at = (hi * LO + lo) * piece
            out_ref[lo, :, hi * piece : (hi + 1) * piece] = x_ref[0, :, at : at + piece]
        for ref in refs[:-1]:
            out_ref[lo, :, HI * piece :] = ref[...]


def unpack_kernel(place_ref, back_ref, *refs):
    out_ref = refs[-1]
    piece = back_ref.shape[2] // HI
    for lo in range(LO):
        for hi in range(HI):
            at = (hi * LO + lo) * piece
            out_ref[0, :, at : at + piece] = back_ref[lo, :, hi * piece : (hi + 1) * piece]


def replicate(tail, first, count, scr, offset, rows, total_rows):
    depth = lax.broadcasted_iota(jnp.int32, (LANES, 2 * LANES), 0)
    side = lax.broadcasted_iota(jnp.int32, (LANES, 2 * LANES), 1) // LANES
    for n in range(0, count, 2):
        column = first + n + side
        pick = ((depth == column) | (depth == 32 + column)).astype(jnp.float32).astype(jnp.bfloat16)
        wide = jnp.dot(tail, pick, preferred_element_type=jnp.float32)
        scr[pl.ds(n * total_rows + offset, rows), :] = wide[:, :LANES]
        scr[pl.ds((n + 1) * total_rows + offset, rows), :] = wide[:, LANES:]


def request_of(place_ref, turn, group):
    return group * 2 + lax.rem(place_ref[3] + turn, 2)


def to_rows(scr, refs, count):
    for p, ref in enumerate(refs):
        for j in range(2):
            value = ref[:, j * LANES : (j + 1) * LANES]
            scr[pl.ds(2 * p + j, count, stride=ROWS), :] = value


def scan_kernel(turn, place_ref, lengths_ref, got_ref, *refs):
    share_ref, refs = (got_ref, refs) if turn == 0 else (refs[0], refs[1:])
    w_refs, decay_refs, bias_refs, skip_refs = (refs[i * HI : (i + 1) * HI] for i in range(4))
    refs = refs[4 * HI :]
    before_refs, refs = refs[:-9], refs[-9:]
    if before_refs:
        leave_ref, seed_refs = before_refs[-1], before_refs[-1 - HI : -1]
        before_refs = before_refs[: -1 - HI]
    y_ref, total_ref, end_ref, step_scr, x_scr, bc_scr, decay_scr, skip_scr, held_scr = refs
    parts, toks, _ = got_ref.shape
    rank, width = w_refs[0].shape
    chans = HI * width
    states = decay_refs[0].shape[0]
    rows = parts * toks
    hi, group = place_ref[0], place_ref[2]
    step_id = pl.program_id(0)

    @pl.when(step_id == 0)
    def _():
        to_rows(decay_scr, decay_refs, states)
        decay_scr[...] = decay_scr[...] * (-LOG2E)
        for p in range(HI):
            for j in range(2):
                skip_scr[2 * p + j : 2 * p + j + 1, :] = skip_refs[p][
                    :, j * LANES : (j + 1) * LANES
                ]
        held_scr[...] = jnp.zeros_like(held_scr)

    wide_x = got_ref[:, :, :chans].reshape(rows, chans).astype(jnp.float32)
    dt = share_ref[:, :, chans : chans + rank].reshape(rows, rank)
    tail = share_ref[:, :, chans + rank :].reshape(rows, LANES)
    position = (hi * pl.num_programs(0) + step_id) * rows + lax.broadcasted_iota(
        jnp.int32, (rows, 1), 0
    )
    live = position < lengths_ref[request_of(place_ref, turn, group)]
    for by in range(HI):
        block = lax.rem(group - by + HI, HI)
        bias = bias_refs[0][...]
        for p in range(1, HI):
            bias = jnp.where(block == p, bias_refs[p][...], bias)
        pre = jnp.dot(dt, w_refs[by][...], preferred_element_type=jnp.float32) + bias
        step = jnp.maximum(pre, 0.0) + jnp.log1p(jnp.exp(-jnp.abs(pre)))
        step = jnp.where(live, step, 0.0)
        for j in range(2):
            step_scr[pl.ds(2 * block + j, rows, stride=ROWS), :] = step[
                :, j * LANES : (j + 1) * LANES
            ]
    for k in range(ROWS):
        x_scr[pl.ds(k, rows, stride=ROWS), :] = wide_x[:, k * LANES : (k + 1) * LANES]
    replicate(tail, 0, 2 * states, bc_scr, 0, rows, rows)
    skip = skip_scr[...]

    def per_tok(tok, carried):
        total, held = carried
        at = pl.ds(pl.multiple_of(tok * ROWS, ROWS), ROWS)
        step = step_scr[at, :]
        wide_x = x_scr[at, :]
        driven = step * wide_x
        total = total + step
        out = skip * wide_x
        new = []
        for n in range(states):
            enter = bc_scr[pl.ds(n * rows + tok, 1), :]
            leave = bc_scr[pl.ds((states + n) * rows + tok, 1), :]
            state = jnp.exp2(step * decay_scr[n * ROWS : (n + 1) * ROWS, :]) * held[n]
            state = state + enter * driven
            out = out + leave * state
            new.append(state)
        total_ref[at, :] = total
        y_ref[at, :] = out
        return total, tuple(new)

    held = tuple(held_scr[n * ROWS : (n + 1) * ROWS, :] for n in range(states))
    total, held = lax.fori_loop(
        0, rows, per_tok, (held_scr[states * ROWS :, :], held), unroll=32
    )
    for n in range(states):
        held_scr[n * ROWS : (n + 1) * ROWS, :] = held[n]
    held_scr[states * ROWS :, :] = total

    @pl.when(step_id == pl.num_programs(0) - 1)
    def _():
        end_ref[...] = held_scr[...]
        if before_refs:
            leave_ref[...] = sent_rows(
                place_ref, list(before_refs) + [held_scr], seed_refs
            )


def sent_rows(place_ref, ends, seed_refs):
    blocks = []
    for ref in ends:
        end = ref[...]
        total = end[-ROWS:]
        top = total.astype(jnp.bfloat16).astype(jnp.float32)
        blocks += [end[:-ROWS], top, total - top]
    seed = sum(ref[...].astype(jnp.float32) for ref in seed_refs)
    states = seed.shape[0] // len(ends)
    seeds = [seed[req * states : (req + 1) * states] for req in range(len(ends))]
    for turn in range(len(ends)):
        mine = jnp.where(request_of(place_ref, turn, 0) == 0, seeds[0], seeds[1])
        for j in range(2):
            blocks.append(mine[:, j * LANES : (j + 1) * LANES])
    return jnp.concatenate(blocks, axis=0).astype(jnp.bfloat16)


def join(place_ref, sent_refs, decay_scr, carry_refs, final_ref, state_scr):
    states = decay_scr.shape[0] // ROWS
    reqs = len(carry_refs)
    hi = place_ref[0]
    per_req = (states + 2) * ROWS
    blocks = [ref[...].astype(jnp.float32) for ref in sent_refs]

    def of_shard(shard, values):
        distance = lax.rem(hi - shard + HI, HI)
        value = values[0]
        for by in range(1, HI):
            value = jnp.where(distance == by, values[by], value)
        return value

    for req in range(reqs):
        ends = [block[req * per_req : (req + 1) * per_req] for block in blocks]
        totals = [end[states * ROWS : (states + 1) * ROWS] + end[(states + 1) * ROWS :] for end in ends]
        in_order = [of_shard(shard, totals) for shard in range(HI)]
        for by, block in enumerate(blocks):
            slot = lax.rem(hi - by + HI, HI)
            for j in range(2):
                at = reqs * per_req + (2 * req + j) * states
                state_scr[pl.ds(2 * slot + j, states, stride=ROWS), :] = block[at : at + states]
        for n in range(states):
            rows = slice(n * ROWS, (n + 1) * ROWS)
            decay = decay_scr[rows, :]
            carry = final = state_scr[rows, :]
            for by in range(HI - 1, 0, -1):
                longer = ends[by][rows] + jnp.exp2(totals[by] * decay) * carry
                carry = jnp.where(hi >= by, longer, carry)
            carry_refs[req][rows, :] = carry
            for shard in range(HI):
                end = of_shard(shard, [end[rows] for end in ends])
                final = end + jnp.exp2(in_order[shard] * decay) * final
            state_scr[rows, :] = final
        for j in range(2):
            value = state_scr[pl.ds(2 * hi + j, states, stride=ROWS), :]
            final_ref[req, :, j * LANES : (j + 1) * LANES] = value.astype(jnp.bfloat16)


def correct_kernel(turn, reqs, place_ref, lengths_ref, y_ref, total_ref, tail_ref, *refs):
    decay_refs, refs = refs[:HI], refs[HI:]
    y_scr, c_scr, decay_scr, carry_scr, state_scr = refs[-5:]
    if turn == 0:
        sent_refs, refs = refs[:HI], refs[HI:]
        out_ref, carry_refs, final_ref = refs[0], refs[1:reqs], refs[reqs]
    else:
        carry_ref, out_ref = refs[:2]
    parts, toks, _ = out_ref.shape
    states = decay_refs[0].shape[0]
    rows = parts * toks
    step_id = pl.program_id(0)

    @pl.when(step_id == 0)
    def _():
        to_rows(decay_scr, decay_refs, states)
        decay_scr[...] = decay_scr[...] * (-LOG2E)
        if turn == 0:
            carries = (carry_scr, *carry_refs)
            join(place_ref, sent_refs, decay_scr, carries, final_ref, state_scr)
        else:
            carry_scr[...] = carry_ref[...]

    replicate(tail_ref[...].reshape(rows, LANES), states, states, c_scr, 0, rows, rows)
    carry = tuple(carry_scr[n * ROWS : (n + 1) * ROWS, :] for n in range(states))

    def per_tok(tok, carry):
        at = pl.ds(pl.multiple_of(tok * ROWS, ROWS), ROWS)
        total = total_ref[at, :]
        out = y_ref[at, :]
        for n in range(states):
            leave = c_scr[pl.ds(n * rows + tok, 1), :]
            decay = decay_scr[n * ROWS : (n + 1) * ROWS, :]
            out = out + leave * (jnp.exp2(total * decay) * carry[n])
        y_scr[at, :] = out
        return carry

    lax.fori_loop(0, rows, per_tok, carry, unroll=32)
    position = (place_ref[0] * pl.num_programs(0) + step_id) * rows + lax.broadcasted_iota(
        jnp.int32, (rows, 1), 0
    )
    live = position < lengths_ref[request_of(place_ref, turn, place_ref[2])]
    for k in range(ROWS):
        block = jnp.where(live, y_scr[pl.ds(k, rows, stride=ROWS), :], 0.0)
        out_ref[:, :, k * LANES : (k + 1) * LANES] = block.astype(jnp.bfloat16).reshape(
            parts, toks, LANES
        )


def shifts(count, by):
    return [(i, (i + by) % count) for i in range(count)]


def on_device(
    conv_out, dt_low, state_proj, dt_weight, dt_bias, decay_rate, skip_gain,
    cache_states, hit_owner, hit_slot, evict_order, new_lengths,
):
    groups = lax.axis_size("cache")
    group = lax.axis_index("cache")
    hi = lax.axis_index("hi")
    lo = lax.axis_index("lo")
    reqs, toks, width = conv_out.shape
    rank = dt_low.shape[2]
    states = decay_rate.shape[0]
    slots, piece = cache_states.shape[0], cache_states.shape[3]
    chans = width // LO
    length = LO * toks
    place = jnp.stack([hi, lo, group, lax.axis_index("head")]).astype(jnp.int32)
    owners = hit_owner[:, 0]
    count = owners.shape[0]
    share_width = rank + LANES

    def exchange(array, axis):
        return lax.all_to_all(array, axis, split_axis=0, concat_axis=0, tiled=True)

    mine = dt_weight.shape[0]
    quarter = pl.pallas_call(
        spread_kernel,
        grid=(1,),
        in_specs=[pl.BlockSpec((mine, width), lambda i: (0, 0))],
        out_specs=pl.BlockSpec((HI * LO, mine, piece), lambda i: (0, 0, 0)),
        out_shape=jax.ShapeDtypeStruct((HI * LO, mine, piece), jnp.bfloat16),
        compiler_params=params(63),
        name="spread",
    )(dt_weight)
    quarter = exchange(quarter, ("hi", "lo")).reshape(rank, piece)

    stored = cache_states.reshape(slots, -1)
    slot_ids = jnp.arange(slots, dtype=jnp.int32)
    wanted = (hit_slot[:, None] == slot_ids[None, :]) & (owners == group)[:, None]
    picked = jnp.dot(
        wanted.astype(jnp.bfloat16), stored, preferred_element_type=jnp.float32
    ).astype(jnp.bfloat16)
    picked = picked.reshape(groups, reqs, states, piece)
    source_group = lax.rem(group - jnp.arange(groups, dtype=jnp.int32) + groups, groups)
    turns = lax.rem(jnp.arange(reqs, dtype=jnp.int32) + place[3], reqs)
    request = (source_group[:, None] * reqs + turns[None, :]).reshape(-1)
    ids = jnp.arange(count, dtype=jnp.int32)
    ranks = jnp.sum((owners[:, None] == owners[None, :]) & (ids[None, :] < ids[:, None]), axis=1)
    target = evict_order[0][ranks]
    hits = (target[request][:, None] == slot_ids[None, :]) & (owners[request] == group)[:, None]

    def of_turn(turn):
        return lambda i, at, *_: (lax.rem(at[3] + turn, 2), 0, 0)

    proj = lax.dynamic_index_in_dim(state_proj, place[3], 0, keepdims=False)
    top = lax.reduce_precision(proj, 8, 7)
    share = jnp.concatenate(
        [
            lax.dynamic_index_in_dim(dt_low, place[3], 0, keepdims=False),
            top.astype(jnp.bfloat16),
            (proj - top).astype(jnp.bfloat16),
            jnp.zeros((toks, LANES - 2 * proj.shape[1]), jnp.bfloat16),
        ],
        axis=1,
    )
    sent_width = chans + share_width
    sent = [
        pl.pallas_call(
            pack_kernel,
            grid_spec=pltpu.PrefetchScalarGridSpec(
                num_scalar_prefetch=1,
                grid=(1,),
                in_specs=[pl.BlockSpec((1, toks, width), of_turn(turn))]
                + [pl.BlockSpec((toks, share_width), lambda i, at: (0, 0))] * (turn == 0),
                out_specs=pl.BlockSpec((LO, toks, columns), lambda i, at: (0, 0, 0)),
            ),
            out_shape=jax.ShapeDtypeStruct((LO, toks, columns), jnp.bfloat16),
            compiler_params=params(63),
            name="pack",
        )(place, conv_out, *[share] * (turn == 0))
        for turn, columns in enumerate((sent_width, chans))
    ]
    first_sent, picked = lax.optimization_barrier((sent[0], picked))

    def wanted_by(member):
        return lax.dynamic_index_in_dim(picked, member, 0, keepdims=False).reshape(-1, piece)

    pieces = [quarter] + [
        lax.ppermute(
            jnp.concatenate([quarter, wanted_by(lax.rem(group + by, groups))]),
            "cache",
            shifts(groups, by),
        )
        for by in range(1, groups)
    ]
    own_seed = wanted_by(group)
    first_got = exchange(first_sent, "lo")
    second_sent, first_got, pieces, hits = lax.optimization_barrier(
        (sent[1], first_got, pieces, hits)
    )
    got = [first_got, exchange(second_sent, "lo")]
    second_share = lax.ppermute(first_got, "head", [(0, 1), (1, 0)])

    steps = 2
    parts = LO // steps
    rows = parts * toks
    rows_f32 = jax.ShapeDtypeStruct((length * ROWS, LANES), jnp.float32)
    rows_spec = pl.BlockSpec((rows * ROWS, LANES), lambda i, *at: (i, 0))
    bias, skip = dt_bias.reshape(1, width), skip_gain.reshape(1, width)

    def whole(*shape):
        return pl.BlockSpec(shape, lambda i, *at: (0,) * len(shape))

    def own(lead):
        return [
            pl.BlockSpec((lead, piece), lambda i, at, *_, p=p: (0, p * LO + at[1]))
            for p in range(HI)
        ]

    def scratch(*lengths):
        return [pltpu.VMEM((n, LANES), jnp.float32) for n in lengths]

    end_rows = (states + 1) * ROWS
    leave_rows = reqs * ((states + 2) * ROWS + 2 * states)
    y, total, end = [], [], []
    for req in range(reqs):
        last = req == reqs - 1
        one_y, one_total, one_end, *leaving = pl.pallas_call(
            functools.partial(scan_kernel, req),
            grid_spec=pltpu.PrefetchScalarGridSpec(
                num_scalar_prefetch=2,
                grid=(steps,),
                in_specs=[
                    pl.BlockSpec((parts, toks, columns), lambda i, *at: (i, 0, 0))
                    for columns in ((chans, sent_width) if req else (sent_width,))
                ]
                + [whole(rank, piece)] * HI
                + own(states)
                + own(1) * 2
                + ([whole(end_rows, LANES)] * req
                   + [whole(reqs * states, piece)]
                   + [pl.BlockSpec((reqs * states, piece), lambda i, *at: (rank // (reqs * states), 0))]
                   * (groups - 1)
                   if last else []),
                out_specs=([whole(leave_rows, LANES)] if last else [])
                + [rows_spec, rows_spec, whole(end_rows, LANES)],
                scratch_shapes=scratch(
                    rows * ROWS, rows * ROWS, 2 * states * rows, states * ROWS, ROWS, end_rows
                ),
            ),
            out_shape=(
                [jax.ShapeDtypeStruct((leave_rows, LANES), jnp.bfloat16)] if last else []
            )
            + [rows_f32, rows_f32, jax.ShapeDtypeStruct((end_rows, LANES), jnp.float32)],
            compiler_params=params(63),
            cost_estimate=cost(15),
            name="scan",
        )(
            place, new_lengths, got[req], *([second_share] if req else []), *pieces, *[decay_rate] * HI, *[bias] * HI,
            *[skip] * HI, *(end + [own_seed, *pieces[1:]] if last else []),
        )
        if last:
            leaving, one_y, one_total, one_end = one_y, one_total, one_end, leaving[0]
        y.append(one_y)
        total.append(one_total)
        end.append(one_end)

    arrived = [lax.ppermute(leaving, "hi", shifts(HI, by)) for by in range(1, HI)]
    carry_rows = states * ROWS
    back, carry = [], None
    for req in range(reqs):
        out, *more = pl.pallas_call(
            functools.partial(correct_kernel, req, reqs),
            grid_spec=pltpu.PrefetchScalarGridSpec(
                num_scalar_prefetch=2,
                grid=(steps,),
                in_specs=[
                    rows_spec,
                    rows_spec,
                    pl.BlockSpec(
                        (parts, toks, LANES), lambda i, *at: (i, 0, (chans + rank) // LANES)
                    ),
                ]
                + own(states)
                + (
                    [whole(carry_rows, LANES)]
                    if req
                    else [whole(leave_rows, LANES)] * HI
                ),
                out_specs=[pl.BlockSpec((parts, toks, chans), lambda i, *at: (i, 0, 0))]
                + (
                    []
                    if req
                    else [whole(carry_rows, LANES)] * (reqs - 1)
                    + [whole(reqs, states, piece)]
                ),
                scratch_shapes=scratch(
                    rows * ROWS, states * rows, carry_rows, carry_rows, carry_rows
                ),
            ),
            out_shape=[jax.ShapeDtypeStruct((LO, toks, chans), jnp.bfloat16)]
            + (
                []
                if req
                else [jax.ShapeDtypeStruct((carry_rows, LANES), jnp.float32)] * (reqs - 1)
                + [jax.ShapeDtypeStruct((reqs, states, piece), jnp.bfloat16)]
            ),
            compiler_params=params(63),
            cost_estimate=cost(9),
            name="correct",
        )(
            place, new_lengths, y[req], total[req], second_share if req else first_got,
            *[decay_rate] * HI, *([carry[req - 1]] if req else [leaving, *arrived]),
        )
        if req == 0:
            carry, held = more[: reqs - 1], more[reqs - 1]
        back.append(exchange(out, "lo"))

    def unpack(turn, mixed):
        return pl.pallas_call(
            unpack_kernel,
            grid_spec=pltpu.PrefetchScalarGridSpec(
                num_scalar_prefetch=1,
                grid=(1,),
                in_specs=[whole(LO, toks, chans)]
                + [pl.BlockSpec(memory_space=pl.ANY)] * len(mixed),
                out_specs=pl.BlockSpec((1, toks, width), of_turn(turn)),
            ),
            out_shape=jax.ShapeDtypeStruct(conv_out.shape, jnp.bfloat16),
            input_output_aliases={2: 0} if mixed else {},
            compiler_params=params(16),
            name="unpack",
        )(place, back[turn], *mixed)

    mixed = unpack(0, [])
    held, mixed = lax.optimization_barrier((held, mixed))

    fresh = [held] + [lax.ppermute(held, "cache", shifts(groups, by)) for by in range(1, groups)]
    fresh = jnp.stack(fresh).reshape(count, -1)
    rows = jnp.dot(
        hits.T.astype(jnp.bfloat16), fresh, preferred_element_type=jnp.float32
    ).astype(jnp.bfloat16)
    updated = jnp.where(jnp.any(hits, axis=0)[:, None], rows, stored)

    updated = updated.reshape(cache_states.shape)
    back[-1], updated = lax.optimization_barrier((back[-1], updated))
    for turn in range(1, reqs):
        mixed = unpack(turn, [mixed])
    return mixed, updated


def solution(mesh):
    fine = Mesh(mesh.devices.reshape(mesh.shape["cache"], HI, LO, mesh.shape["head"]),
                ("cache", "hi", "lo", "head"))
    ctx = ("hi", "lo")
    in_specs = (
        P("cache", ctx, "head"),
        P("cache", ctx, None),
        P("cache", ctx, None),
        P(ctx, "head"),
        P("head"),
        P(None, "head"),
        P("head"),
        P("cache", "head", None, ctx),
        P(),
        P(),
        P("cache", None),
        P(),
    )
    out_specs = (P("cache", ctx, "head"), P("cache", "head", None, ctx))
    return jax.shard_map(
        on_device, mesh=fine, in_specs=in_specs, out_specs=out_specs, check_vma=False
    )
```

```python
import functools
import math

import jax
import jax.numpy as jnp
from jax import lax
from jax.experimental import pallas as pl
from jax.experimental.pallas import tpu as pltpu
from jax.sharding import Mesh, PartitionSpec as P

HI, LO = 4, 8
LANES, ROWS = 128, 8
LOG2E = math.log2(math.e)


def params(mib):
    return pltpu.CompilerParams(vmem_limit_bytes=mib << 20)


def cost(us):
    return pl.CostEstimate(flops=0, bytes_accessed=int(us * 3.6e6), transcendentals=0)


def spread_kernel(w_ref, out_ref):
    piece = w_ref.shape[1] // (HI * LO)
    first = lax.axis_index("cache") * (LO * piece)
    for lo in range(LO):
        block = w_ref[:, pl.ds(pl.multiple_of(first + lo * piece, piece), piece)]
        for hi in range(HI):
            out_ref[hi * LO + lo] = block


def pack_kernel(place_ref, x_ref, *refs):
    out_ref = refs[-1]
    piece = x_ref.shape[2] // (HI * LO)
    for lo in range(LO):
        for hi in range(HI):
            at = (hi * LO + lo) * piece
            out_ref[lo, :, hi * piece : (hi + 1) * piece] = x_ref[0, :, at : at + piece]
        for ref in refs[:-1]:
            out_ref[lo, :, HI * piece :] = ref[...]


def unpack_kernel(place_ref, back_ref, *refs):
    out_ref = refs[-1]
    piece = back_ref.shape[2] // HI
    for lo in range(LO):
        for hi in range(HI):
            at = (hi * LO + lo) * piece
            out_ref[0, :, at : at + piece] = back_ref[lo, :, hi * piece : (hi + 1) * piece]


def replicate(tail, first, count, scr, offset, rows, total_rows):
    depth = lax.broadcasted_iota(jnp.int32, (LANES, 2 * LANES), 0)
    side = lax.broadcasted_iota(jnp.int32, (LANES, 2 * LANES), 1) // LANES
    for n in range(0, count, 2):
        column = first + n + side
        pick = ((depth == column) | (depth == 32 + column)).astype(jnp.float32).astype(jnp.bfloat16)
        wide = jnp.dot(tail, pick, preferred_element_type=jnp.float32)
        scr[pl.ds(n * total_rows + offset, rows), :] = wide[:, :LANES]
        scr[pl.ds((n + 1) * total_rows + offset, rows), :] = wide[:, LANES:]


def request_of(place_ref, turn, group):
    return group * 2 + lax.rem(place_ref[3] + turn, 2)


def to_rows(scr, refs, count):
    for p, ref in enumerate(refs):
        for j in range(2):
            value = ref[:, j * LANES : (j + 1) * LANES]
            scr[pl.ds(2 * p + j, count, stride=ROWS), :] = value


def scan_kernel(turn, place_ref, lengths_ref, got_ref, *refs):
    share_ref, refs = (got_ref, refs) if turn == 0 else (refs[0], refs[1:])
    w_refs, decay_refs, bias_refs, skip_refs = (refs[i * HI : (i + 1) * HI] for i in range(4))
    refs = refs[4 * HI :]
    before_refs, refs = refs[:-9], refs[-9:]
    if before_refs:
        leave_ref, seed_refs = before_refs[-1], before_refs[-1 - HI : -1]
        before_refs = before_refs[: -1 - HI]
    y_ref, total_ref, end_ref, step_scr, x_scr, bc_scr, decay_scr, skip_scr, held_scr = refs
    parts, toks, _ = got_ref.shape
    rank, width = w_refs[0].shape
    chans = HI * width
    states = decay_refs[0].shape[0]
    rows = parts * toks
    hi, group = place_ref[0], place_ref[2]
    step_id = pl.program_id(0)

    @pl.when(step_id == 0)
    def _():
        to_rows(decay_scr, decay_refs, states)
        decay_scr[...] = decay_scr[...] * (-LOG2E)
        for p in range(HI):
            for j in range(2):
                skip_scr[2 * p + j : 2 * p + j + 1, :] = skip_refs[p][
                    :, j * LANES : (j + 1) * LANES
                ]
        held_scr[...] = jnp.zeros_like(held_scr)

    wide_x = got_ref[:, :, :chans].reshape(rows, chans).astype(jnp.float32)
    dt = share_ref[:, :, chans : chans + rank].reshape(rows, rank)
    tail = share_ref[:, :, chans + rank :].reshape(rows, LANES)
    position = (hi * pl.num_programs(0) + step_id) * rows + lax.broadcasted_iota(
        jnp.int32, (rows, 1), 0
    )
    live = position < lengths_ref[request_of(place_ref, turn, group)]
    for by in range(HI):
        block = lax.rem(group - by + HI, HI)
        bias = bias_refs[0][...]
        for p in range(1, HI):
            bias = jnp.where(block == p, bias_refs[p][...], bias)
        pre = jnp.dot(dt, w_refs[by][...], preferred_element_type=jnp.float32) + bias
        step = jnp.maximum(pre, 0.0) + jnp.log1p(jnp.exp(-jnp.abs(pre)))
        step = jnp.where(live, step, 0.0)
        for j in range(2):
            step_scr[pl.ds(2 * block + j, rows, stride=ROWS), :] = step[
                :, j * LANES : (j + 1) * LANES
            ]
    for k in range(ROWS):
        x_scr[pl.ds(k, rows, stride=ROWS), :] = wide_x[:, k * LANES : (k + 1) * LANES]
    replicate(tail, 0, 2 * states, bc_scr, 0, rows, rows)
    skip = skip_scr[...]

    def per_tok(tok, carried):
        total, held = carried
        at = pl.ds(pl.multiple_of(tok * ROWS, ROWS), ROWS)
        step = step_scr[at, :]
        wide_x = x_scr[at, :]
        driven = step * wide_x
        total = total + step
        out = skip * wide_x
        new = []
        for n in range(states):
            enter = bc_scr[pl.ds(n * rows + tok, 1), :]
            leave = bc_scr[pl.ds((states + n) * rows + tok, 1), :]
            state = jnp.exp2(step * decay_scr[n * ROWS : (n + 1) * ROWS, :]) * held[n]
            state = state + enter * driven
            out = out + leave * state
            new.append(state)
        total_ref[at, :] = total
        y_ref[at, :] = out
        return total, tuple(new)

    held = tuple(held_scr[n * ROWS : (n + 1) * ROWS, :] for n in range(states))
    total, held = lax.fori_loop(
        0, rows, per_tok, (held_scr[states * ROWS :, :], held), unroll=32
    )
    for n in range(states):
        held_scr[n * ROWS : (n + 1) * ROWS, :] = held[n]
    held_scr[states * ROWS :, :] = total

    @pl.when(step_id == pl.num_programs(0) - 1)
    def _():
        end_ref[...] = held_scr[...]
        if before_refs:
            leave_ref[...] = sent_rows(
                place_ref, list(before_refs) + [held_scr], seed_refs
            )


def sent_rows(place_ref, ends, seed_refs):
    blocks = []
    for ref in ends:
        end = ref[...]
        total = end[-ROWS:]
        top = total.astype(jnp.bfloat16).astype(jnp.float32)
        blocks += [end[:-ROWS], top, total - top]
    seed = sum(ref[...].astype(jnp.float32) for ref in seed_refs)
    states = seed.shape[0] // len(ends)
    seeds = [seed[req * states : (req + 1) * states] for req in range(len(ends))]
    for turn in range(len(ends)):
        mine = jnp.where(request_of(place_ref, turn, 0) == 0, seeds[0], seeds[1])
        for j in range(2):
            blocks.append(mine[:, j * LANES : (j + 1) * LANES])
    return jnp.concatenate(blocks, axis=0).astype(jnp.bfloat16)


def join(place_ref, reqs, turn, sent_refs, decay_scr, carry_scr, final_ref, state_scr):
    states = decay_scr.shape[0] // ROWS
    hi = place_ref[0]
    per_req = (states + 2) * ROWS
    blocks = [ref[...].astype(jnp.float32) for ref in sent_refs]

    def of_shard(shard, values):
        distance = lax.rem(hi - shard + HI, HI)
        value = values[0]
        for by in range(1, HI):
            value = jnp.where(distance == by, values[by], value)
        return value

    for req in range(reqs) if final_ref is not None else [turn]:
        ends = [block[req * per_req : (req + 1) * per_req] for block in blocks]
        totals = [end[states * ROWS : (states + 1) * ROWS] + end[(states + 1) * ROWS :] for end in ends]
        in_order = [of_shard(shard, totals) for shard in range(HI)]
        for by, block in enumerate(blocks):
            slot = lax.rem(hi - by + HI, HI)
            for j in range(2):
                at = reqs * per_req + (2 * req + j) * states
                state_scr[pl.ds(2 * slot + j, states, stride=ROWS), :] = block[at : at + states]
        for n in range(states):
            rows = slice(n * ROWS, (n + 1) * ROWS)
            decay = decay_scr[rows, :]
            carry = final = state_scr[rows, :]
            if req == turn:
                for by in range(HI - 1, 0, -1):
                    longer = ends[by][rows] + jnp.exp2(totals[by] * decay) * carry
                    carry = jnp.where(hi >= by, longer, carry)
                carry_scr[rows, :] = carry
            if final_ref is None:
                continue
            for shard in range(HI):
                end = of_shard(shard, [end[rows] for end in ends])
                final = end + jnp.exp2(in_order[shard] * decay) * final
            state_scr[rows, :] = final
        for j in range(2 if final_ref is not None else 0):
            value = state_scr[pl.ds(2 * hi + j, states, stride=ROWS), :]
            final_ref[req, :, j * LANES : (j + 1) * LANES] = value.astype(jnp.bfloat16)


def columns_kernel(states, tail_ref, out_ref):
    rows = tail_ref.shape[0] * tail_ref.shape[1]
    replicate(tail_ref[...].reshape(rows, LANES), states, states, out_ref, 0, rows, rows)


def correct_kernel(turn, reqs, place_ref, lengths_ref, y_ref, total_ref, tail_ref, *refs):
    decay_refs, refs = refs[:HI], refs[HI:]
    y_scr, c_scr, decay_scr, carry_scr, state_scr = refs[-5:]
    sent_refs, out_ref = refs[:HI], refs[HI]
    final_ref = refs[HI + 1] if turn == reqs - 1 else None
    parts, toks, _ = out_ref.shape
    states = decay_refs[0].shape[0]
    rows = parts * toks
    step_id = pl.program_id(0)

    @pl.when(step_id == 0)
    def _():
        to_rows(decay_scr, decay_refs, states)
        decay_scr[...] = decay_scr[...] * (-LOG2E)
        join(place_ref, reqs, turn, sent_refs, decay_scr, carry_scr, final_ref, state_scr)

    if turn == 0:
        c_scr = tail_ref
    else:
        replicate(tail_ref[...].reshape(rows, LANES), states, states, c_scr, 0, rows, rows)
    carry = tuple(carry_scr[n * ROWS : (n + 1) * ROWS, :] for n in range(states))

    def per_tok(tok, carry):
        at = pl.ds(pl.multiple_of(tok * ROWS, ROWS), ROWS)
        total = total_ref[at, :]
        out = y_ref[at, :]
        for n in range(states):
            leave = c_scr[pl.ds(n * rows + tok, 1), :]
            decay = decay_scr[n * ROWS : (n + 1) * ROWS, :]
            out = out + leave * (jnp.exp2(total * decay) * carry[n])
        y_scr[at, :] = out
        return carry

    lax.fori_loop(0, rows, per_tok, carry, unroll=32)
    position = (place_ref[0] * pl.num_programs(0) + step_id) * rows + lax.broadcasted_iota(
        jnp.int32, (rows, 1), 0
    )
    live = position < lengths_ref[request_of(place_ref, turn, place_ref[2])]
    for k in range(ROWS):
        block = jnp.where(live, y_scr[pl.ds(k, rows, stride=ROWS), :], 0.0)
        out_ref[:, :, k * LANES : (k + 1) * LANES] = block.astype(jnp.bfloat16).reshape(
            parts, toks, LANES
        )


def shifts(count, by):
    return [(i, (i + by) % count) for i in range(count)]


def on_device(
    conv_out, dt_low, state_proj, dt_weight, dt_bias, decay_rate, skip_gain,
    cache_states, hit_owner, hit_slot, evict_order, new_lengths,
):
    groups = lax.axis_size("cache")
    group = lax.axis_index("cache")
    hi = lax.axis_index("hi")
    lo = lax.axis_index("lo")
    reqs, toks, width = conv_out.shape
    rank = dt_low.shape[2]
    states = decay_rate.shape[0]
    slots, piece = cache_states.shape[0], cache_states.shape[3]
    chans = width // LO
    length = LO * toks
    place = jnp.stack([hi, lo, group, lax.axis_index("head")]).astype(jnp.int32)
    owners = hit_owner[:, 0]
    count = owners.shape[0]
    share_width = rank + LANES

    def exchange(array, axis):
        return lax.all_to_all(array, axis, split_axis=0, concat_axis=0, tiled=True)

    mine = dt_weight.shape[0]
    quarter = pl.pallas_call(
        spread_kernel,
        grid=(1,),
        in_specs=[pl.BlockSpec((mine, width), lambda i: (0, 0))],
        out_specs=pl.BlockSpec((HI * LO, mine, piece), lambda i: (0, 0, 0)),
        out_shape=jax.ShapeDtypeStruct((HI * LO, mine, piece), jnp.bfloat16),
        compiler_params=params(63),
        name="spread",
    )(dt_weight)
    quarter = exchange(quarter, ("hi", "lo")).reshape(rank, piece)

    stored = cache_states.reshape(slots, -1)
    slot_ids = jnp.arange(slots, dtype=jnp.int32)
    wanted = (hit_slot[:, None] == slot_ids[None, :]) & (owners == group)[:, None]
    picked = jnp.dot(
        wanted.astype(jnp.bfloat16), stored, preferred_element_type=jnp.float32
    ).astype(jnp.bfloat16)
    picked = picked.reshape(groups, reqs, states, piece)
    source_group = lax.rem(group - jnp.arange(groups, dtype=jnp.int32) + groups, groups)
    turns = lax.rem(jnp.arange(reqs, dtype=jnp.int32) + place[3], reqs)
    request = (source_group[:, None] * reqs + turns[None, :]).reshape(-1)
    ids = jnp.arange(count, dtype=jnp.int32)
    ranks = jnp.sum((owners[:, None] == owners[None, :]) & (ids[None, :] < ids[:, None]), axis=1)
    target = evict_order[0][ranks]
    hits = (target[request][:, None] == slot_ids[None, :]) & (owners[request] == group)[:, None]

    def of_turn(turn):
        return lambda i, at, *_: (lax.rem(at[3] + turn, 2), 0, 0)

    proj = lax.dynamic_index_in_dim(state_proj, place[3], 0, keepdims=False)
    top = lax.reduce_precision(proj, 8, 7)
    share = jnp.concatenate(
        [
            lax.dynamic_index_in_dim(dt_low, place[3], 0, keepdims=False),
            top.astype(jnp.bfloat16),
            (proj - top).astype(jnp.bfloat16),
            jnp.zeros((toks, LANES - 2 * proj.shape[1]), jnp.bfloat16),
        ],
        axis=1,
    )
    sent_width = chans + share_width
    sent = [
        pl.pallas_call(
            pack_kernel,
            grid_spec=pltpu.PrefetchScalarGridSpec(
                num_scalar_prefetch=1,
                grid=(1,),
                in_specs=[pl.BlockSpec((1, toks, width), of_turn(turn))]
                + [pl.BlockSpec((toks, share_width), lambda i, at: (0, 0))] * (turn == 0),
                out_specs=pl.BlockSpec((LO, toks, columns), lambda i, at: (0, 0, 0)),
            ),
            out_shape=jax.ShapeDtypeStruct((LO, toks, columns), jnp.bfloat16),
            compiler_params=params(63),
            name="pack",
        )(place, conv_out, *[share] * (turn == 0))
        for turn, columns in enumerate((sent_width, chans))
    ]
    first_sent, picked = lax.optimization_barrier((sent[0], picked))

    def wanted_by(member):
        return lax.dynamic_index_in_dim(picked, member, 0, keepdims=False).reshape(-1, piece)

    pieces = [quarter] + [
        lax.ppermute(
            jnp.concatenate([quarter, wanted_by(lax.rem(group + by, groups))]),
            "cache",
            shifts(groups, by),
        )
        for by in range(1, groups)
    ]
    own_seed = wanted_by(group)
    first_got = exchange(first_sent, "lo")
    second_sent, first_got, pieces, hits = lax.optimization_barrier(
        (sent[1], first_got, pieces, hits)
    )
    got = [first_got, exchange(second_sent, "lo")]
    second_share = lax.ppermute(first_got, "head", [(0, 1), (1, 0)])

    steps = 2
    parts = LO // steps
    rows = parts * toks
    rows_f32 = jax.ShapeDtypeStruct((length * ROWS, LANES), jnp.float32)
    rows_spec = pl.BlockSpec((rows * ROWS, LANES), lambda i, *at: (i, 0))
    bias, skip = dt_bias.reshape(1, width), skip_gain.reshape(1, width)

    def whole(*shape):
        return pl.BlockSpec(shape, lambda i, *at: (0,) * len(shape))

    def own(lead):
        return [
            pl.BlockSpec((lead, piece), lambda i, at, *_, p=p: (0, p * LO + at[1]))
            for p in range(HI)
        ]

    def scratch(*lengths):
        return [pltpu.VMEM((n, LANES), jnp.float32) for n in lengths]

    end_rows = (states + 1) * ROWS
    leave_rows = reqs * ((states + 2) * ROWS + 2 * states)
    y, total, end = [], [], []
    for req in range(reqs):
        last = req == reqs - 1
        one_y, one_total, one_end, *leaving = pl.pallas_call(
            functools.partial(scan_kernel, req),
            grid_spec=pltpu.PrefetchScalarGridSpec(
                num_scalar_prefetch=2,
                grid=(steps,),
                in_specs=[
                    pl.BlockSpec((parts, toks, columns), lambda i, *at: (i, 0, 0))
                    for columns in ((chans, sent_width) if req else (sent_width,))
                ]
                + [whole(rank, piece)] * HI
                + own(states)
                + own(1) * 2
                + ([whole(end_rows, LANES)] * req
                   + [whole(reqs * states, piece)]
                   + [pl.BlockSpec((reqs * states, piece), lambda i, *at: (rank // (reqs * states), 0))]
                   * (groups - 1)
                   if last else []),
                out_specs=([whole(leave_rows, LANES)] if last else [])
                + [rows_spec, rows_spec, whole(end_rows, LANES)],
                scratch_shapes=scratch(
                    rows * ROWS, rows * ROWS, 2 * states * rows, states * ROWS, ROWS, end_rows
                ),
            ),
            out_shape=(
                [jax.ShapeDtypeStruct((leave_rows, LANES), jnp.bfloat16)] if last else []
            )
            + [rows_f32, rows_f32, jax.ShapeDtypeStruct((end_rows, LANES), jnp.float32)],
            compiler_params=params(63),
            cost_estimate=cost(15),
            name="scan",
        )(
            place, new_lengths, got[req], *([second_share] if req else []), *pieces, *[decay_rate] * HI, *[bias] * HI,
            *[skip] * HI, *(end + [own_seed, *pieces[1:]] if last else []),
        )
        if last:
            leaving, one_y, one_total, one_end = one_y, one_total, one_end, leaving[0]
        y.append(one_y)
        total.append(one_total)
        end.append(one_end)

    carry_rows = states * ROWS
    late_got, leaving = lax.optimization_barrier((first_got, leaving))
    arrived = [lax.ppermute(leaving, "hi", shifts(HI, by)) for by in range(1, HI)]
    tail_spec = pl.BlockSpec((parts, toks, LANES), lambda i, *at: (i, 0, (chans + rank) // LANES))
    columns_spec = pl.BlockSpec((states * rows, LANES), lambda i, *at: (i, 0))
    columns = pl.pallas_call(
        functools.partial(columns_kernel, states),
        grid=(steps,),
        in_specs=[tail_spec],
        out_specs=columns_spec,
        out_shape=jax.ShapeDtypeStruct((steps * states * rows, LANES), jnp.float32),
        compiler_params=params(63),
        cost_estimate=cost(4),
        name="columns",
    )(late_got)
    back = []
    for req in range(reqs):
        out, *more = pl.pallas_call(
            functools.partial(correct_kernel, req, reqs),
            grid_spec=pltpu.PrefetchScalarGridSpec(
                num_scalar_prefetch=2,
                grid=(steps,),
                in_specs=[
                    rows_spec,
                    rows_spec,
                    tail_spec if req else columns_spec,
                ]
                + own(states)
                + [whole(leave_rows, LANES)] * HI,
                out_specs=[pl.BlockSpec((parts, toks, chans), lambda i, *at: (i, 0, 0))]
                + [whole(reqs, states, piece)] * (req == reqs - 1),
                scratch_shapes=scratch(
                    rows * ROWS, states * rows, carry_rows, carry_rows, carry_rows
                ),
            ),
            out_shape=[jax.ShapeDtypeStruct((LO, toks, chans), jnp.bfloat16)]
            + [jax.ShapeDtypeStruct((reqs, states, piece), jnp.bfloat16)] * (req == reqs - 1),
            compiler_params=params(63),
            cost_estimate=cost(9),
            name="correct",
        )(
            place, new_lengths, y[req], total[req], second_share if req else columns,
            *[decay_rate] * HI, leaving, *arrived,
        )
        held = more[0] if more else None
        back.append(exchange(out, "lo"))

    def unpack(turn, mixed):
        return pl.pallas_call(
            unpack_kernel,
            grid_spec=pltpu.PrefetchScalarGridSpec(
                num_scalar_prefetch=1,
                grid=(2,),
                in_specs=[pl.BlockSpec((LO, toks // 2, chans), lambda i, at: (0, i, 0))]
                + [pl.BlockSpec(memory_space=pl.ANY)] * len(mixed),
                out_specs=pl.BlockSpec(
                    (1, toks // 2, width), lambda i, at: (lax.rem(at[3] + turn, 2), i, 0)
                ),
            ),
            out_shape=jax.ShapeDtypeStruct(conv_out.shape, jnp.bfloat16),
            input_output_aliases={2: 0} if mixed else {},
            compiler_params=params(16),
            name="unpack",
        )(place, back[turn], *mixed)

    mixed = unpack(0, [])
    held, mixed = lax.optimization_barrier((held, mixed))

    fresh = [held] + [lax.ppermute(held, "cache", shifts(groups, by)) for by in range(1, groups)]
    fresh = jnp.stack(fresh).reshape(count, -1)
    rows = jnp.dot(
        hits.T.astype(jnp.bfloat16), fresh, preferred_element_type=jnp.float32
    ).astype(jnp.bfloat16)
    updated = jnp.where(jnp.any(hits, axis=0)[:, None], rows, stored)

    updated = updated.reshape(cache_states.shape)
    back[-1], updated = lax.optimization_barrier((back[-1], updated))
    for turn in range(1, reqs):
        mixed = unpack(turn, [mixed])
    return mixed, updated


def solution(mesh):
    fine = Mesh(mesh.devices.reshape(mesh.shape["cache"], HI, LO, mesh.shape["head"]),
                ("cache", "hi", "lo", "head"))
    ctx = ("hi", "lo")
    in_specs = (
        P("cache", ctx, "head"),
        P("cache", ctx, None),
        P("cache", ctx, None),
        P(ctx, "head"),
        P("head"),
        P(None, "head"),
        P("head"),
        P("cache", "head", None, ctx),
        P(),
        P(),
        P("cache", None),
        P(),
    )
    out_specs = (P("cache", ctx, "head"), P("cache", "head", None, ctx))
    return jax.shard_map(
        on_device, mesh=fine, in_specs=in_specs, out_specs=out_specs, check_vma=False
    )
```
